768 devices in a mesh: gx: 192 (over y, z, core), gy: 4 (over x).
Axes of the slice: x: 4, y: 8, z: 12, core: 2. Of those that a mesh axis runs over, the one named last changes fastest.
Arguments:
- adjoint_source: float32 [2, 11, 1536, 512], P(None, None, 'gx', 'gy'), may hold values from -80 to 80, as said below
- viscosity: float32 [11, 1536, 512], P(None, 'gx', 'gy'), may hold values from 0.3 to 3
- friction: float32 [1536, 512], P('gx', 'gy'), may hold values from 0.1 to 10
- ice_mask: int32 [1536, 512], P('gx', 'gy'), may hold values 0 or 1
Outputs:
- adjoint_velocity: float32 [2, 11, 1536, 512], P(None, None, 'gx', 'gy')
- residual: float32 [2, 11, 1536, 512], P(None, None, 'gx', 'gy')
The draws below stay inside these ranges and needn't reach their ends.
Inputs may be any that keep to these rules, and one draw needn't show every extreme that they name: `adjoint_source`: rough from column to column, of varying scale.
All inputs are finite; a program needn't handle non-finite values. No bound on the sum of `ice_mask` on one device may be relied on, other than what follows from the above.
Results may differ from the reference program's by a relative error of at most 0.006.
Values sent between devices are 32-bit elements; how exact they have to be, the bound alone decides.
No kernel may reach another device: no remote copies, remote signals or barrier semaphores. Data moves between devices by JAX's collectives and lax.ppermute only.
A program may use at most 32 MiB of HBM per device.

```python
import math
import jax
import jax.numpy as jnp
import numpy as np
from jax import lax

LEVELS = 11
ITERS = 3
CX = 8
NX = 1536
NY = 512


def draw_adjoint_source(key, part):
    key = jax.random.fold_in(key, 11)
    key_base, key_cols = jax.random.split(key, 2)
    shape = (2, LEVELS, NX, NY)
    base = jnp.clip(jax.random.normal(key_base, shape, jnp.float32), -8.0, 8.0)
    ramp = 1.0 + 2.0 * jnp.arange(NX, dtype=jnp.float32) / max(NX - 1, 1)
    column_scale = jnp.exp(jax.random.uniform(key_cols, (NX, NY), jnp.float32) * math.log(10.0)) / 3.0
    return base * ramp[None, None, :, None] * column_scale[None, None]


def plant(result, own_key, smallest, high):
    shape = result.shape
    place = [jax.random.randint(jax.random.fold_in(own_key, axis), (), 0, shape[axis]) for axis in range(len(shape))]
    result = result.at[tuple(place)].set(smallest)
    longest = shape.index(max(shape))
    place[longest] = (place[longest] + 1) % shape[longest]
    return result.at[tuple(place)].set(high)


def level_of(rng, dims, cuts, low, high):
    gain = 1.0
    for position, parts in cuts:
        heights = jax.random.uniform(jax.random.fold_in(jax.random.fold_in(rng, 6), position), (parts,), jnp.float32, low / len(cuts), high / len(cuts))
        gain = gain * jnp.repeat(jnp.exp(heights), dims[position] // parts).reshape((-1,) + (1,) * (len(dims) - 1 - position))
    return gain


def setup_inputs(seed: int = 0) -> dict:
    keys = jax.random.split(jax.random.key(seed), 5)
    adjoint_source = draw_adjoint_source(jax.random.fold_in(keys[4], 71), 0)
    viscosity = jnp.clip(jnp.exp(math.log(3.0) - 2.3025851 * jax.random.uniform(keys[1], (LEVELS, NX, NY), jnp.float32) ** level_of(keys[1], (LEVELS, NX, NY), ((1, 192), (2, 4)), -0.2, 0.2)), 0.3, 3.0)
    friction = jnp.clip(jnp.exp(math.log(10.0) - 4.6051702 * jax.random.uniform(keys[2], (NX, NY), jnp.float32) ** level_of(keys[2], (NX, NY), ((0, 192), (1, 4)), -0.2, 0.2)), 0.1, 10.0)
    ice_mask = plant((jax.random.randint(keys[3], (NX, NY), 0, 8) < 7).astype(jnp.int32), jax.random.fold_in(keys[3], 1), 0, 1)
    return dict(adjoint_source=adjoint_source, viscosity=viscosity, friction=friction, ice_mask=ice_mask)


vertical_weight = 4.0

def corner_offsets():
    return [(upper_z, upper_x, upper_y) for upper_z in (0, 1) for upper_x in (0, 1) for upper_y in (0, 1)]

def element_table():
    gauss_points = [0.5 - 0.5 / math.sqrt(3.0), 0.5 + 0.5 / math.sqrt(3.0)]
    corner_list = corner_offsets()
    gradients = np.zeros((3, 8, 8))
    for quad_index, quad_corner in enumerate(corner_list):
        coords = [gauss_points[picked] for picked in quad_corner]
        for node_index, node_corner in enumerate(corner_list):
            factors = [coords[axis_index] if node_corner[axis_index] else 1.0 - coords[axis_index] for axis_index in range(3)]
            slopes = [1.0 if node_corner[axis_index] else -1.0 for axis_index in range(3)]
            gradients[0, node_index, quad_index] = slopes[1] * factors[0] * factors[2]
            gradients[1, node_index, quad_index] = slopes[2] * factors[0] * factors[1]
            gradients[2, node_index, quad_index] = slopes[0] * factors[1] * factors[2]
    pairs = np.zeros((3, 3, 8, 8))
    for first_axis in range(3):
        for second_axis in range(3):
            for node_index in range(8):
                for other_index in range(8):
                    total = 0.0
                    for quad_index in range(8):
                        total += gradients[first_axis, node_index, quad_index] * gradients[second_axis, other_index, quad_index]
                    pairs[first_axis, second_axis, node_index, other_index] = total / 8.0
    along_uu = 4.0 * pairs[0, 0] + pairs[1, 1] + vertical_weight * pairs[2, 2]
    along_vv = pairs[0, 0] + 4.0 * pairs[1, 1] + vertical_weight * pairs[2, 2]
    coupled = 2.0 * pairs[0, 1] + pairs[1, 0]
    table = np.zeros((16, 16))
    table[0:8, 0:8] = along_uu
    table[0:8, 8:16] = coupled
    table[8:16, 0:8] = np.transpose(coupled)
    table[8:16, 8:16] = along_vv
    return table.astype(np.float32)

def cell_residual(padded, eta_padded):
    layers = padded.shape[1] - 1
    cells_x = padded.shape[2] - 1
    cells_y = padded.shape[3] - 1
    corner_list = corner_offsets()
    pieces = []
    for component in (0, 1):
        for upper_z, upper_x, upper_y in corner_list:
            pieces.append(padded[component, upper_z:upper_z + layers, upper_x:upper_x + cells_x, upper_y:upper_y + cells_y])
    stacked = jnp.stack(pieces)
    eta_cells = eta_padded[0:layers, 0:cells_x, 0:cells_y]
    for upper_z, upper_x, upper_y in corner_list[1:]:
        eta_cells = eta_cells + eta_padded[upper_z:upper_z + layers, upper_x:upper_x + cells_x, upper_y:upper_y + cells_y]
    eta_cells = eta_cells * 0.125
    table = jnp.asarray(element_table(), dtype=padded.dtype)
    products = jnp.einsum('ij,jlxy->ilxy', table, stacked, precision=lax.Precision.HIGHEST) * eta_cells[None]
    outputs = []
    for component in (0, 1):
        summed = jnp.zeros(padded.shape[1:], padded.dtype)
        for corner_index, (upper_z, upper_x, upper_y) in enumerate(corner_list):
            summed = summed + jnp.pad(products[component * 8 + corner_index], ((upper_z, 1 - upper_z), (upper_x, 1 - upper_x), (upper_y, 1 - upper_y)))
        outputs.append(summed)
    return jnp.stack(outputs)

def apply_operator(field, viscosity, friction, weights):
    padded = jnp.pad(field, ((0, 0), (0, 0), (1, 1), (1, 1)))
    eta_padded = jnp.pad(viscosity, ((0, 0), (1, 1), (1, 1)))

    def one_block(block_index):
        start = block_index * CX
        piece = lax.dynamic_slice_in_dim(padded, start, CX + 2, 2)
        eta_piece = lax.dynamic_slice_in_dim(eta_padded, start, CX + 2, 1)
        return cell_residual(piece, eta_piece)[:, :, 1:-1, 1:-1]
    block_parts = lax.map(one_block, jnp.arange(NX // CX, dtype=jnp.int32))
    stiffness = jnp.moveaxis(block_parts, 0, 2).reshape(2, LEVELS, NX, NY)
    bed_rows = stiffness[:, 0] + friction[None] * field[:, 0]
    stiffness = stiffness.at[:, 0].set(bed_rows)
    return stiffness * weights

def reference(adjoint_source, viscosity, friction, ice_mask):
    weights = ice_mask.astype(adjoint_source.dtype)[None, None]
    residual = adjoint_source * weights
    adjoint_velocity = jnp.zeros_like(residual)
    direction = residual
    norm_now = jnp.sum(residual * residual)
    for iteration in range(ITERS):
        image = apply_operator(direction, viscosity, friction, weights)
        alpha = norm_now / jnp.sum(direction * image)
        adjoint_velocity = adjoint_velocity + alpha * direction
        residual = residual - alpha * image
        norm_next = jnp.sum(residual * residual)
        direction = residual + norm_next / norm_now * direction
        norm_now = norm_next
    return (adjoint_velocity, residual)
```

```python
import jax
import jax.numpy as jnp
from jax import lax
from jax.experimental import pallas as pl
from jax.experimental.pallas import tpu as pltpu
from jax.sharding import Mesh, PartitionSpec as P

LEVELS = 11
FIELDS = 3 * LEVELS + 2
SCALE = 16.0
SHIFTS = (8.0, 2.0, 20.0)
F32 = jnp.float32
VMEM = pltpu.VMEM

MASS = {"s": 0.25, "d": 1.0 / 12.0}
SLOPE = {"s": 0.0, "d": 1.0}


def field_list(src_ref, eta_ref, fric_ref, mask_ref):
    fields = [src_ref[c, l] for c in (0, 1) for l in range(LEVELS)]
    fields += [eta_ref[l] for l in range(LEVELS)]
    fields += [fric_ref[...], mask_ref[...].astype(F32)]
    return fields


def pack_kernel(src_ref, eta_ref, fric_ref, mask_ref, low_ref, high_ref, down_ref, up_ref):
    lane = lax.broadcasted_iota(jnp.int32, (8, 128), 1)
    low = jnp.zeros((8, 128), F32)
    high = jnp.zeros((8, 128), F32)
    for f, value in enumerate(field_list(src_ref, eta_ref, fric_ref, mask_ref)):
        place = (lane >= 3 * f) & (lane < 3 * f + 3)
        low = jnp.where(place, pltpu.roll(value, 3 * f, 1) if f else value, low)
        high = jnp.where(place, pltpu.roll(value, (3 * f - 125) % 128, 1), high)
        down_ref[f] = value[0:4]
        up_ref[f] = value[4:8]
    low_ref[...] = low
    high_ref[...] = high
    for f in (FIELDS, FIELDS + 1):
        down_ref[f] = jnp.zeros((4, 128), F32)
        up_ref[f] = jnp.zeros((4, 128), F32)


def ahead(value, axis):
    return pltpu.roll(value, value.shape[axis] - 1, axis)


def behind(value, axis):
    return pltpu.roll(value, 1, axis)


def coefficient(mode, cx, cy, cz):
    x, y, z = mode
    total = cx * SLOPE[x] * MASS[y] * MASS[z]
    total += cy * MASS[x] * SLOPE[y] * MASS[z]
    return total + cz * MASS[x] * MASS[y] * SLOPE[z]


def flat_modes(plane):
    after = ahead(plane, 1)
    s, d = plane + after, after - plane
    s1, d1 = ahead(s, 0), ahead(d, 0)
    return {"ss": s + s1, "ds": s1 - s, "sd": d + d1, "dd": d1 - d}


def flat_back(modes):
    s = modes["ss"] - modes["ds"] + behind(modes["ss"] + modes["ds"], 0)
    d = modes["sd"] - modes["dd"] + behind(modes["sd"] + modes["dd"], 0)
    return s - d + behind(s + d, 1)


def layer(lower, upper, eta):
    modes = []
    for c in (0, 1):
        m = {}
        for xy in ("ss", "ds", "sd", "dd"):
            m[xy + "d"] = upper[c][xy] - lower[c][xy]
            if xy != "ss":
                m[xy + "s"] = upper[c][xy] + lower[c][xy]
        modes.append(m)
    low, high = [], []
    for c in (0, 1):
        weights = (4.0, 1.0, 4.0) if c == 0 else (1.0, 4.0, 4.0)
        own, other = modes[c], modes[1 - c]
        out = {}
        for m, value in own.items():
            out[m] = coefficient(m, *weights) * value
        for z in "sd":
            q = 0.25 * MASS[z]
            double, single = ("ds", "sd") if c == 0 else ("sd", "ds")
            out[double + z] = out[double + z] + (2.0 * q) * other[single + z]
            out[single + z] = out[single + z] + q * other[double + z]
        out = {m: value * eta for m, value in out.items()}
        lo, hi = {}, {}
        for xy in ("ss", "ds", "sd", "dd"):
            d = out[xy + "d"]
            s = out.get(xy + "s")
            lo[xy] = -d if s is None else s - d
            hi[xy] = d if s is None else s + d
        low.append(lo)
        high.append(hi)
    return low, high


def krylov_kernel(
    src_ref, eta_ref, fric_ref, mask_ref, left_ref, right_ref, next_ref, prev_ref,
    out_ref, row_ref, vec, cell, frict, mask,
):
    lane = lax.broadcasted_iota(jnp.int32, (16, 128), 1)
    left = jnp.concatenate([left_ref[...], next_ref[FIELDS + 1], prev_ref[FIELDS + 1]], 0)
    right = jnp.concatenate([right_ref[...], next_ref[FIELDS], prev_ref[FIELDS]], 0)
    fields = field_list(src_ref, eta_ref, fric_ref, mask_ref)

    def plane(f):
        own = jnp.concatenate([fields[f], next_ref[f], prev_ref[f]], 0)
        from_left = pltpu.roll(left, (125 - 3 * f) % 128, 1)
        from_right = pltpu.roll(right, (-3 * f) % 128, 1) if f else right
        zero = jnp.zeros((16, 128), F32)
        side = jnp.where(lane >= 125, from_left, jnp.where(lane < 3, from_right, zero))
        return jnp.concatenate([own, side], 1)

    frict[...] = plane(3 * LEVELS) * (1.0 / SCALE)
    mask_plane = plane(3 * LEVELS + 1)
    mask[...] = mask_plane
    for l in range(LEVELS):
        vec[0, 0, l] = plane(l) * mask_plane
        vec[0, 1, l] = plane(LEVELS + l) * mask_plane
    below = None
    for l in range(LEVELS):
        value = plane(2 * LEVELS + l)
        value = value + ahead(value, 1)
        value = value + ahead(value, 0)
        if below is not None:
            cell[l - 1] = (below + value) * (0.125 / SCALE)
        below = value

    for k in range(3):
        shift = SHIFTS[k] / SCALE

        def finish(l, sums):
            for c in (0, 1):
                value = vec[k, c, l]
                image = flat_back(sums[c])
                if l == 0:
                    image = image + frict[...] * value
                vec[k + 1, c, l] = image * mask[...] - shift * value

        lower = [flat_modes(vec[k, c, 0]) for c in (0, 1)]
        pending = None
        for l in range(LEVELS - 1):
            upper = [flat_modes(vec[k, c, l + 1]) for c in (0, 1)]
            low, high = layer(lower, upper, cell[l])
            if pending is not None:
                low = [{m: low[c][m] + pending[c][m] for m in low[c]} for c in (0, 1)]
            finish(l, low)
            lower, pending = upper, high
        finish(LEVELS - 1, pending)

    pairs = ((0, 0), (0, 1), (0, 2), (1, 1), (1, 2), (2, 2), (1, 3), (2, 3))
    sums = [jnp.zeros((8, 128), F32) for _ in pairs]
    for c in (0, 1):
        for l in range(LEVELS):
            v = [vec[k, c, l, 0:8, 0:128] for k in range(4)]
            for k in range(4):
                out_ref[k, c, l] = v[k]
            sums = [s + v[i] * v[j] for s, (i, j) in zip(sums, pairs)]
    stacked = jnp.concatenate([jnp.sum(s, axis=0, keepdims=True) for s in sums], 0)
    totals = jnp.sum(stacked, axis=1, keepdims=True)
    ids = [lax.broadcasted_iota(jnp.int32, (8, 128), a) for a in (0, 1)]
    spread = jnp.where(ids[0] == ids[1], totals, 0.0)
    row_ref[...] = jnp.sum(spread, axis=0, keepdims=True)


def coordinates(gram):
    def dot(a, b):
        total = None
        for i in range(len(a)):
            for j in range(len(b)):
                term = a[i] * b[j] * gram[min(i, j), max(i, j)]
                total = term if total is None else total + term
        return total

    def added(a, b, factor):
        size = max(len(a), len(b))
        out = []
        for i in range(size):
            if i >= len(b):
                out.append(a[i])
            elif i >= len(a):
                out.append(factor * b[i])
            else:
                out.append(a[i] + factor * b[i])
        return out

    one = jnp.ones_like(gram[0, 0])
    residual, direction, answer = [one], [one], []
    norm = gram[0, 0]
    for k in range(3):
        image = [SHIFTS[i] * direction[i] for i in range(k + 1)] + [SCALE * direction[k]]
        for i in range(1, k + 1):
            image[i] = image[i] + SCALE * direction[i - 1]
        alpha = norm / dot(direction, image)
        answer = added(answer, direction, alpha)
        residual = added(residual, image, -alpha)
        if k < 2:
            fresh = dot(residual, residual)
            direction = added(residual, direction, fresh / norm)
            norm = fresh
    return answer, residual


def combine_kernel(vec_ref, rows_ref, answer_ref, residual_ref):
    row = jnp.sum(rows_ref[...], axis=0, keepdims=True)
    ids = [lax.broadcasted_iota(jnp.int32, (8, 128), a) for a in (0, 1)]
    totals = jnp.sum(jnp.where(ids[0] == ids[1], row, 0.0), axis=1, keepdims=True)
    tile = jnp.broadcast_to(totals, (8, 128))
    pairs = ((0, 0), (0, 1), (0, 2), (1, 1), (1, 2), (2, 2), (1, 3), (2, 3))
    gram = {pair: tile[n : n + 1] for n, pair in enumerate(pairs)}
    gram[0, 3] = gram[1, 2] + ((SHIFTS[0] - SHIFTS[2]) / SCALE) * gram[0, 2]
    answer, residual = coordinates(gram)
    answer = [jnp.broadcast_to(a, (8, 128)) for a in answer]
    residual = [jnp.broadcast_to(a, (8, 128)) for a in residual]
    for c in (0, 1):
        for l in range(LEVELS):
            v = [vec_ref[k, c, l] for k in range(4)]
            answer_ref[c, l] = answer[0] * v[0] + answer[1] * v[1] + answer[2] * v[2]
            residual_ref[c, l] = (
                residual[0] * v[0] + residual[1] * v[1] + residual[2] * v[2] + residual[3] * v[3]
            )


def vmem(n):
    return [pl.BlockSpec(memory_space=VMEM)] * n


def shape(*dims):
    return jax.ShapeDtypeStruct(dims, F32)


def everywhere(row, axes):
    size = lax.axis_size(axes)
    spread = jnp.broadcast_to(row[None], (size, 1, 128))
    return lax.all_to_all(spread, axes, 0, 0, tiled=True)


def local(adjoint_source, viscosity, friction, ice_mask):
    gx, gy = ("far", "near"), "gy"
    size_x, size_y = lax.axis_size(gx), lax.axis_size(gy)
    fields = (adjoint_source, viscosity, friction, ice_mask)
    low, high, down, up = pl.pallas_call(
        pack_kernel,
        out_shape=(shape(8, 128), shape(8, 128), shape(FIELDS + 2, 4, 128), shape(FIELDS + 2, 4, 128)),
        in_specs=vmem(4),
        out_specs=tuple(vmem(4)),
    )(*fields)
    right = lax.ppermute(low, gy, [(i + 1, i) for i in range(size_y - 1)])
    left = lax.ppermute(high, gy, [(i, i + 1) for i in range(size_y - 1)])
    down = down.at[FIELDS:].set(jnp.stack([right[0:4], left[0:4]]))
    up = up.at[FIELDS:].set(jnp.stack([right[4:8], left[4:8]]))
    following = lax.ppermute(down, gx, [(i + 1, i) for i in range(size_x - 1)])
    previous = lax.ppermute(up, gx, [(i, i + 1) for i in range(size_x - 1)])
    vectors, row = pl.pallas_call(
        krylov_kernel,
        out_shape=(shape(4, 2, LEVELS, 8, 128), shape(1, 128)),
        in_specs=vmem(8),
        out_specs=tuple(vmem(2)),
        scratch_shapes=[
            VMEM((4, 2, LEVELS, 16, 256), F32),
            VMEM((LEVELS - 1, 16, 256), F32),
            VMEM((16, 256), F32),
            VMEM((16, 256), F32),
        ],
    )(*fields, left, right, following, previous)
    row = jnp.sum(everywhere(row, "near"), axis=0)
    rows = everywhere(row, ("far", "gy"))[:, 0]
    return pl.pallas_call(
        combine_kernel,
        out_shape=(shape(2, LEVELS, 8, 128), shape(2, LEVELS, 8, 128)),
        in_specs=vmem(2),
        out_specs=tuple(vmem(2)),
    )(vectors, rows)


def solution(mesh):
    size_x, size_y = mesh.devices.shape
    split = Mesh(mesh.devices.reshape(8, size_x // 8, size_y), ("far", "near", "gy"))
    gx = ("far", "near")
    vector, plane = P(None, None, gx, "gy"), P(gx, "gy")
    return jax.shard_map(
        local,
        mesh=split,
        in_specs=(vector, P(None, gx, "gy"), plane, plane),
        out_specs=(vector, vector),
        check_vma=False,
    )
```

```python
import jax
import jax.numpy as jnp
from jax import lax
from jax.experimental import pallas as pl
from jax.experimental.pallas import tpu as pltpu
from jax.sharding import Mesh, PartitionSpec as P

LEVELS = 11
FIELDS = 3 * LEVELS + 2
SCALE = 16.0
SHIFTS = (8.0, 2.0, 20.0)
F32 = jnp.float32
VMEM = pltpu.VMEM

MASS = {"s": 0.25, "d": 1.0 / 12.0}
SLOPE = {"s": 0.0, "d": 1.0}


def side_kernel(src_ref, eta_ref, fric_ref, mask_ref, fields_ref, low_ref, high_ref, mask, sems):
    parts = [
        (src_ref.at[0], fields_ref.at[0:LEVELS]),
        (src_ref.at[1], fields_ref.at[LEVELS : 2 * LEVELS]),
        (eta_ref, fields_ref.at[2 * LEVELS : 3 * LEVELS]),
        (fric_ref, fields_ref.at[3 * LEVELS]),
        (mask_ref, mask),
    ]
    copies = [pltpu.make_async_copy(a, b, sems.at[n]) for n, (a, b) in enumerate(parts)]
    for copy in copies:
        copy.start()
    for copy in copies:
        copy.wait()
    fields_ref[FIELDS - 1] = mask[...].astype(F32)
    lane = lax.broadcasted_iota(jnp.int32, (8, 128), 1)
    low = jnp.zeros((8, 128), F32)
    high = jnp.zeros((8, 128), F32)
    for f in range(FIELDS):
        value = fields_ref[f]
        place = (lane >= 3 * f) & (lane < 3 * f + 3)
        low = jnp.where(place, pltpu.roll(value, 3 * f, 1) if f else value, low)
        high = jnp.where(place, pltpu.roll(value, (3 * f - 125) % 128, 1), high)
    low_ref[...] = low
    high_ref[...] = high


def rows_kernel(fields_ref, right_ref, left_ref, down_ref, up_ref):
    for f in range(FIELDS):
        value = fields_ref[f]
        down_ref[f] = value[0:4]
        up_ref[f] = value[4:8]
    for f, value in ((FIELDS, right_ref[...]), (FIELDS + 1, left_ref[...])):
        down_ref[f] = value[0:4]
        up_ref[f] = value[4:8]


def ahead(value, axis):
    return pltpu.roll(value, value.shape[axis] - 1, axis)


def behind(value, axis):
    return pltpu.roll(value, 1, axis)


def coefficient(mode, cx, cy, cz):
    x, y, z = mode
    total = cx * SLOPE[x] * MASS[y] * MASS[z]
    total += cy * MASS[x] * SLOPE[y] * MASS[z]
    return total + cz * MASS[x] * MASS[y] * SLOPE[z]


def flat_modes(plane):
    after = ahead(plane, 1)
    s, d = plane + after, after - plane
    s1, d1 = ahead(s, 0), ahead(d, 0)
    return {"ss": s + s1, "ds": s1 - s, "sd": d + d1, "dd": d1 - d}


def flat_back(modes):
    s = modes["ss"] - modes["ds"] + behind(modes["ss"] + modes["ds"], 0)
    d = modes["sd"] - modes["dd"] + behind(modes["sd"] + modes["dd"], 0)
    return s - d + behind(s + d, 1)


def layer(lower, upper, eta):
    modes = []
    for c in (0, 1):
        m = {}
        for xy in ("ss", "ds", "sd", "dd"):
            m[xy + "d"] = upper[c][xy] - lower[c][xy]
            if xy != "ss":
                m[xy + "s"] = upper[c][xy] + lower[c][xy]
        modes.append(m)
    low, high = [], []
    for c in (0, 1):
        weights = (4.0, 1.0, 4.0) if c == 0 else (1.0, 4.0, 4.0)
        own, other = modes[c], modes[1 - c]
        out = {}
        for m, value in own.items():
            out[m] = coefficient(m, *weights) * value
        for z in "sd":
            q = 0.25 * MASS[z]
            double, single = ("ds", "sd") if c == 0 else ("sd", "ds")
            out[double + z] = out[double + z] + (2.0 * q) * other[single + z]
            out[single + z] = out[single + z] + q * other[double + z]
        out = {m: value * eta for m, value in out.items()}
        lo, hi = {}, {}
        for xy in ("ss", "ds", "sd", "dd"):
            d = out[xy + "d"]
            s = out.get(xy + "s")
            lo[xy] = -d if s is None else s - d
            hi[xy] = d if s is None else s + d
        low.append(lo)
        high.append(hi)
    return low, high


def krylov_kernel(
    fields_ref, left_ref, right_ref, next_ref, prev_ref,
    out_ref, row_ref, vec, cell, frict, mask,
):
    lane = lax.broadcasted_iota(jnp.int32, (16, 128), 1)
    left = jnp.concatenate([left_ref[...], next_ref[FIELDS + 1], prev_ref[FIELDS + 1]], 0)
    right = jnp.concatenate([right_ref[...], next_ref[FIELDS], prev_ref[FIELDS]], 0)
    def plane(f):
        own = jnp.concatenate([fields_ref[f], next_ref[f], prev_ref[f]], 0)
        from_left = pltpu.roll(left, (125 - 3 * f) % 128, 1)
        from_right = pltpu.roll(right, (-3 * f) % 128, 1) if f else right
        zero = jnp.zeros((16, 128), F32)
        side = jnp.where(lane >= 125, from_left, jnp.where(lane < 3, from_right, zero))
        return jnp.concatenate([own, side], 1)

    frict[...] = plane(3 * LEVELS) * (1.0 / SCALE)
    mask_plane = plane(3 * LEVELS + 1)
    mask[...] = mask_plane
    for l in range(LEVELS):
        vec[0, 0, l] = plane(l) * mask_plane
        vec[0, 1, l] = plane(LEVELS + l) * mask_plane
    below = None
    for l in range(LEVELS):
        value = plane(2 * LEVELS + l)
        value = value + ahead(value, 1)
        value = value + ahead(value, 0)
        if below is not None:
            cell[l - 1] = (below + value) * (0.125 / SCALE)
        below = value

    for k in range(3):
        shift = SHIFTS[k] / SCALE

        def finish(l, sums):
            for c in (0, 1):
                value = vec[k, c, l]
                image = flat_back(sums[c])
                if l == 0:
                    image = image + frict[...] * value
                vec[k + 1, c, l] = image * mask[...] - shift * value

        lower = [flat_modes(vec[k, c, 0]) for c in (0, 1)]
        pending = None
        for l in range(LEVELS - 1):
            upper = [flat_modes(vec[k, c, l + 1]) for c in (0, 1)]
            low, high = layer(lower, upper, cell[l])
            if pending is not None:
                low = [{m: low[c][m] + pending[c][m] for m in low[c]} for c in (0, 1)]
            finish(l, low)
            lower, pending = upper, high
        finish(LEVELS - 1, pending)

    pairs = ((0, 0), (0, 1), (0, 2), (1, 1), (1, 2), (2, 2), (1, 3), (2, 3))
    sums = [jnp.zeros((8, 128), F32) for _ in pairs]
    for c in (0, 1):
        for l in range(LEVELS):
            v = [vec[k, c, l, 0:8, 0:128] for k in range(4)]
            for k in range(4):
                out_ref[k, c, l] = v[k]
            sums = [s + v[i] * v[j] for s, (i, j) in zip(sums, pairs)]
    stacked = jnp.concatenate([jnp.sum(s, axis=0, keepdims=True) for s in sums], 0)
    totals = jnp.sum(stacked, axis=1, keepdims=True)
    ids = [lax.broadcasted_iota(jnp.int32, (8, 128), a) for a in (0, 1)]
    spread = jnp.where(ids[0] == ids[1], totals, 0.0)
    row_ref[...] = jnp.sum(spread, axis=0, keepdims=True)


def coordinates(gram):
    def dot(a, b):
        total = None
        for i in range(len(a)):
            for j in range(len(b)):
                term = a[i] * b[j] * gram[min(i, j), max(i, j)]
                total = term if total is None else total + term
        return total

    def added(a, b, factor):
        size = max(len(a), len(b))
        out = []
        for i in range(size):
            if i >= len(b):
                out.append(a[i])
            elif i >= len(a):
                out.append(factor * b[i])
            else:
                out.append(a[i] + factor * b[i])
        return out

    one = jnp.ones_like(gram[0, 0])
    residual, direction, answer = [one], [one], []
    norm = gram[0, 0]
    for k in range(3):
        image = [SHIFTS[i] * direction[i] for i in range(k + 1)] + [SCALE * direction[k]]
        for i in range(1, k + 1):
            image[i] = image[i] + SCALE * direction[i - 1]
        alpha = norm / dot(direction, image)
        answer = added(answer, direction, alpha)
        residual = added(residual, image, -alpha)
        if k < 2:
            fresh = dot(residual, residual)
            direction = added(residual, direction, fresh / norm)
            norm = fresh
    return answer, residual


def combine_kernel(vec_ref, rows_ref, answer_ref, residual_ref):
    row = jnp.sum(rows_ref[...], axis=0, keepdims=True)
    ids = [lax.broadcasted_iota(jnp.int32, (8, 128), a) for a in (0, 1)]
    totals = jnp.sum(jnp.where(ids[0] == ids[1], row, 0.0), axis=1, keepdims=True)
    tile = jnp.broadcast_to(totals, (8, 128))
    pairs = ((0, 0), (0, 1), (0, 2), (1, 1), (1, 2), (2, 2), (1, 3), (2, 3))
    gram = {pair: tile[n : n + 1] for n, pair in enumerate(pairs)}
    gram[0, 3] = gram[1, 2] + ((SHIFTS[0] - SHIFTS[2]) / SCALE) * gram[0, 2]
    answer, residual = coordinates(gram)
    answer = [jnp.broadcast_to(a, (8, 128)) for a in answer]
    residual = [jnp.broadcast_to(a, (8, 128)) for a in residual]
    for c in (0, 1):
        for l in range(LEVELS):
            v = [vec_ref[k, c, l] for k in range(4)]
            answer_ref[c, l] = answer[0] * v[0] + answer[1] * v[1] + answer[2] * v[2]
            residual_ref[c, l] = (
                residual[0] * v[0] + residual[1] * v[1] + residual[2] * v[2] + residual[3] * v[3]
            )


def call(kernel, outs, megabytes, *scratch, space=VMEM):
    def run(*args):
        return pl.pallas_call(
            kernel,
            out_shape=tuple(outs),
            in_specs=[pl.BlockSpec(memory_space=space)] * len(args),
            out_specs=tuple([pl.BlockSpec(memory_space=VMEM)] * len(outs)),
            scratch_shapes=list(scratch),
            compiler_params=pltpu.CompilerParams(vmem_limit_bytes=megabytes << 20),
        )(*args)

    return run


def shape(*dims):
    return jax.ShapeDtypeStruct(dims, F32)


def everywhere(row, axes):
    size = lax.axis_size(axes)
    spread = jnp.broadcast_to(row[None], (size, 1, 128))
    return lax.all_to_all(spread, axes, 0, 0, tiled=True)


def local(*arguments):
    gx, gy = ("far", "near"), "gy"
    size_x, size_y = lax.axis_size(gx), lax.axis_size(gy)
    fields, low, high = call(
        side_kernel,
        [shape(FIELDS, 8, 128), shape(8, 128), shape(8, 128)],
        2,
        VMEM((8, 128), jnp.int32),
        pltpu.SemaphoreType.DMA((5,)),
        space=pltpu.HBM,
    )(*[pltpu.with_memory_space_constraint(a, pltpu.HBM) for a in arguments])
    left = lax.ppermute(high, gy, [(i, i + 1) for i in range(size_y - 1)])
    right = lax.ppermute(low, gy, [(i + 1, i) for i in range(size_y - 1)])
    down, up = call(rows_kernel, [shape(FIELDS + 2, 4, 128)] * 2, 2)(fields, right, left)
    following = lax.ppermute(down, gx, [(i + 1, i) for i in range(size_x - 1)])
    previous = lax.ppermute(up, gx, [(i, i + 1) for i in range(size_x - 1)])
    vectors, row = call(
        krylov_kernel,
        [shape(4, 2, LEVELS, 8, 128), shape(1, 128)],
        8,
        VMEM((4, 2, LEVELS, 16, 256), F32),
        VMEM((LEVELS - 1, 16, 256), F32),
        VMEM((16, 256), F32),
        VMEM((16, 256), F32),
    )(fields, left, right, following, previous)
    row = jnp.sum(everywhere(row, "near"), axis=0)
    rows = everywhere(row, ("far", "gy"))[:, 0]
    return call(combine_kernel, [shape(2, LEVELS, 8, 128)] * 2, 4)(vectors, rows)


def solution(mesh):
    size_x, size_y = mesh.devices.shape
    split = Mesh(mesh.devices.reshape(8, size_x // 8, size_y), ("far", "near", "gy"))
    gx = ("far", "near")
    vector, plane = P(None, None, gx, "gy"), P(gx, "gy")
    return jax.shard_map(
        local,
        mesh=split,
        in_specs=(vector, P(None, gx, "gy"), plane, plane),
        out_specs=(vector, vector),
        check_vma=False,
    )
```

```python
import jax
import jax.numpy as jnp
from jax import lax
from jax.experimental import pallas as pl
from jax.experimental.pallas import tpu as pltpu
from jax.sharding import Mesh, PartitionSpec as P

LEVELS = 11
FIELDS = 3 * LEVELS + 2
SCALE = 16.0
SHIFTS = (8.0, 2.0, 20.0)
FACTORS = (1.0, 2.0, 4.0, 1.0 / 3.0, 2.0 / 3.0, 5.0 / 3.0)
F32 = jnp.float32
VMEM = pltpu.VMEM


def side_kernel(src_ref, eta_ref, fric_ref, mask_ref, fields_ref, low_ref, high_ref, mask, sems):
    parts = [
        (src_ref.at[0], fields_ref.at[0:LEVELS]),
        (src_ref.at[1], fields_ref.at[LEVELS : 2 * LEVELS]),
        (eta_ref, fields_ref.at[2 * LEVELS : 3 * LEVELS]),
        (fric_ref, fields_ref.at[3 * LEVELS]),
        (mask_ref, mask),
    ]
    copies = [pltpu.make_async_copy(a, b, sems.at[n]) for n, (a, b) in enumerate(parts)]
    for copy in copies:
        copy.start()
    for copy in copies:
        copy.wait()
    fields_ref[FIELDS - 1] = mask[...].astype(F32)
    lane = lax.broadcasted_iota(jnp.int32, (8, 128), 1)
    low = jnp.zeros((8, 128), F32)
    high = jnp.zeros((8, 128), F32)
    for f in range(FIELDS):
        value = fields_ref[f]
        place = (lane >= 3 * f) & (lane < 3 * f + 3)
        low = jnp.where(place, pltpu.roll(value, 3 * f, 1) if f else value, low)
        high = jnp.where(place, pltpu.roll(value, (3 * f - 125) % 128, 1), high)
    low_ref[...] = low
    high_ref[...] = high


def rows_kernel(fields_ref, right_ref, left_ref, down_ref, up_ref):
    for f in range(FIELDS):
        value = fields_ref[f]
        down_ref[f] = value[0:4]
        up_ref[f] = value[4:8]
    for f, value in ((FIELDS, right_ref[...]), (FIELDS + 1, left_ref[...])):
        down_ref[f] = value[0:4]
        up_ref[f] = value[4:8]


def ahead(value, axis):
    return pltpu.roll(value, value.shape[axis] - 1, axis)


def behind(value, axis):
    return pltpu.roll(value, 1, axis)


def flat_modes(plane, after):
    s, d = plane + after, after - plane
    s1, d1 = ahead(s, 0), ahead(d, 0)
    return {"ss": s + s1, "ds": s1 - s, "sd": d + d1, "dd": d1 - d}


def flat_back(modes):
    s = modes["ss"] - modes["ds"] + behind(modes["ss"] + modes["ds"], 0)
    d = modes["sd"] - modes["dd"] + behind(modes["sd"] + modes["dd"], 0)
    return s - d, s + d


def layer(lower, upper, eta):
    whole, double, four, third, two_thirds, five_thirds = eta
    modes = []
    for c in (0, 1):
        m = {}
        for xy in ("ss", "ds", "sd", "dd"):
            m[xy + "d"] = upper[c][xy] - lower[c][xy]
            if xy != "ss":
                m[xy + "s"] = upper[c][xy] + lower[c][xy]
        modes.append(m)
    low, high = [], []
    for c in (0, 1):
        u, v = modes[c], modes[1 - c]
        first, second = ("ds", "sd") if c == 0 else ("sd", "ds")
        up = {
            first + "s": double * (u[first + "s"] + u[first + "s"] + v[second + "s"]),
            second + "s": whole * (u[second + "s"] + v[first + "s"]),
            first + "d": two_thirds * (4.0 * u[first + "d"] + v[second + "d"]),
            second + "d": third * (5.0 * u[second + "d"] + v[first + "d"]),
            "dds": five_thirds * u["dds"],
            "ddd": whole * u["ddd"],
        }
        ssd = four * u["ssd"]
        lo, hi = {"ss": -ssd}, {"ss": ssd}
        for xy in ("ds", "sd", "dd"):
            lo[xy] = up[xy + "s"] - up[xy + "d"]
            hi[xy] = up[xy + "s"] + up[xy + "d"]
        low.append(lo)
        high.append(hi)
    return low, high


def krylov_kernel(
    fields_ref, left_ref, right_ref, next_ref, prev_ref,
    out_ref, row_ref, vec, eta, cell, after, near, far, frict, mask,
):
    lane = lax.broadcasted_iota(jnp.int32, (16, 128), 1)
    left = jnp.concatenate([left_ref[...], next_ref[FIELDS + 1], prev_ref[FIELDS + 1]], 0)
    right = jnp.concatenate([right_ref[...], next_ref[FIELDS], prev_ref[FIELDS]], 0)
    def plane(f):
        own = jnp.concatenate([fields_ref[f], next_ref[f], prev_ref[f]], 0)
        from_left = pltpu.roll(left, (125 - 3 * f) % 128, 1)
        from_right = pltpu.roll(right, (-3 * f) % 128, 1) if f else right
        zero = jnp.zeros((16, 128), F32)
        side = jnp.where(lane >= 125, from_left, jnp.where(lane < 3, from_right, zero))
        return jnp.concatenate([own, side], 1)

    for l in range(LEVELS):
        eta[l] = plane(2 * LEVELS + l)
    mask[...] = plane(3 * LEVELS + 1)
    frict[...] = plane(3 * LEVELS) * (1.0 / SCALE)
    for l in range(LEVELS):
        vec[0, 0, l] = plane(l)
        vec[0, 1, l] = plane(LEVELS + l)
    for l in range(LEVELS - 1):
        value = (eta[l] + eta[l + 1]) * (0.125 / SCALE / 16.0)
        cell[0, l] = value + ahead(value, 1)
    for l in range(LEVELS - 1):
        value = cell[0, l] + ahead(cell[0, l], 0)
        for n, factor in enumerate(FACTORS):
            cell[n, l] = factor * value
    for l in range(LEVELS):
        for c in (0, 1):
            vec[0, c, l] = vec[0, c, l] * mask[...]

    for k in range(3):
        shift = SHIFTS[k] / SCALE

        for c in (0, 1):
            for l in range(LEVELS):
                after[c, l] = ahead(vec[k, c, l], 1)
        for side in (slice(0, 128), slice(128, 256)):
            lower, pending = None, None
            for l in range(LEVELS):
                upper = [
                    flat_modes(vec[k, c, l, :, side], after[c, l, :, side]) for c in (0, 1)
                ]
                if l:
                    eta_parts = [cell[n, l - 1, :, side] for n in range(len(FACTORS))]
                    sums, high = layer(lower, upper, eta_parts)
                    if pending is not None:
                        sums = [{m: sums[c][m] + pending[c][m] for m in sums[c]} for c in (0, 1)]
                    for c in (0, 1):
                        near[c, l - 1, :, side], far[c, l - 1, :, side] = flat_back(sums[c])
                    pending = high
                lower = upper
            for c in (0, 1):
                near[c, LEVELS - 1, :, side], far[c, LEVELS - 1, :, side] = flat_back(pending[c])
        for c in (0, 1):
            for l in range(LEVELS):
                if k < 2:
                    image = near[c, l] + behind(far[c, l], 1)
                    value = vec[k, c, l]
                    if l == 0:
                        image = image + frict[...] * value
                    vec[k + 1, c, l] = image * mask[...] - shift * value
                else:
                    image = near[c, l, 0:8, 0:128] + behind(far[c, l, 0:8], 1)[:, 0:128]
                    value = vec[k, c, l, 0:8, 0:128]
                    if l == 0:
                        image = image + frict[0:8, 0:128] * value
                    vec[k + 1, c, l, 0:8, 0:128] = image * mask[0:8, 0:128] - shift * value

    pairs = ((0, 0), (0, 1), (0, 2), (1, 1), (1, 2), (2, 2), (1, 3), (2, 3))
    sums = [jnp.zeros((8, 128), F32) for _ in pairs]
    for c in (0, 1):
        for l in range(LEVELS):
            v = [vec[k, c, l, 0:8, 0:128] for k in range(4)]
            for k in range(4):
                out_ref[k, c, l] = v[k]
            sums = [s + v[i] * v[j] for s, (i, j) in zip(sums, pairs)]
    stacked = jnp.concatenate([jnp.sum(s, axis=0, keepdims=True) for s in sums], 0)
    totals = jnp.sum(stacked, axis=1, keepdims=True)
    ids = [lax.broadcasted_iota(jnp.int32, (8, 128), a) for a in (0, 1)]
    spread = jnp.where(ids[0] == ids[1], totals, 0.0)
    row_ref[...] = jnp.sum(spread, axis=0, keepdims=True)


def coordinates(gram):
    def dot(a, b):
        total = None
        for i in range(len(a)):
            for j in range(len(b)):
                term = a[i] * b[j] * gram[min(i, j), max(i, j)]
                total = term if total is None else total + term
        return total

    def added(a, b, factor):
        size = max(len(a), len(b))
        out = []
        for i in range(size):
            if i >= len(b):
                out.append(a[i])
            elif i >= len(a):
                out.append(factor * b[i])
            else:
                out.append(a[i] + factor * b[i])
        return out

    one = jnp.ones_like(gram[0, 0])
    residual, direction, answer = [one], [one], []
    norm = gram[0, 0]
    for k in range(3):
        image = [SHIFTS[i] * direction[i] for i in range(k + 1)] + [SCALE * direction[k]]
        for i in range(1, k + 1):
            image[i] = image[i] + SCALE * direction[i - 1]
        alpha = norm / dot(direction, image)
        answer = added(answer, direction, alpha)
        residual = added(residual, image, -alpha)
        if k < 2:
            fresh = dot(residual, residual)
            direction = added(residual, direction, fresh / norm)
            norm = fresh
    return answer, residual


def combine_kernel(vec_ref, rows_ref, answer_ref, residual_ref):
    row = jnp.sum(rows_ref[...], axis=0, keepdims=True)
    ids = [lax.broadcasted_iota(jnp.int32, (8, 128), a) for a in (0, 1)]
    totals = jnp.sum(jnp.where(ids[0] == ids[1], row, 0.0), axis=1, keepdims=True)
    tile = jnp.broadcast_to(totals, (8, 128))
    pairs = ((0, 0), (0, 1), (0, 2), (1, 1), (1, 2), (2, 2), (1, 3), (2, 3))
    gram = {pair: tile[n : n + 1] for n, pair in enumerate(pairs)}
    gram[0, 3] = gram[1, 2] + ((SHIFTS[0] - SHIFTS[2]) / SCALE) * gram[0, 2]
    answer, residual = coordinates(gram)
    answer = [jnp.broadcast_to(a, (8, 128)) for a in answer]
    residual = [jnp.broadcast_to(a, (8, 128)) for a in residual]
    for c in (0, 1):
        for l in range(LEVELS):
            v = [vec_ref[k, c, l] for k in range(4)]
            answer_ref[c, l] = answer[0] * v[0] + answer[1] * v[1] + answer[2] * v[2]
            residual_ref[c, l] = (
                residual[0] * v[0] + residual[1] * v[1] + residual[2] * v[2] + residual[3] * v[3]
            )


def call(kernel, outs, megabytes, *scratch, space=VMEM):
    def run(*args):
        return pl.pallas_call(
            kernel,
            out_shape=tuple(outs),
            in_specs=[pl.BlockSpec(memory_space=space)] * len(args),
            out_specs=tuple([pl.BlockSpec(memory_space=VMEM)] * len(outs)),
            scratch_shapes=list(scratch),
            compiler_params=pltpu.CompilerParams(vmem_limit_bytes=megabytes << 20),
        )(*args)

    return run


def shape(*dims):
    return jax.ShapeDtypeStruct(dims, F32)


def everywhere(row, axes):
    size = lax.axis_size(axes)
    spread = jnp.broadcast_to(row[None], (size, 1, 128))
    return lax.all_to_all(spread, axes, 0, 0, tiled=True)


def local(*arguments):
    gx, gy = ("far", "near"), "gy"
    size_x, size_y = lax.axis_size(gx), lax.axis_size(gy)
    fields, low, high = call(
        side_kernel,
        [shape(FIELDS, 8, 128), shape(8, 128), shape(8, 128)],
        2,
        VMEM((8, 128), jnp.int32),
        pltpu.SemaphoreType.DMA((5,)),
        space=pltpu.HBM,
    )(*[pltpu.with_memory_space_constraint(a, pltpu.HBM) for a in arguments])
    odd_y = lax.axis_index(gy) % 2 == 1
    middle = [(i, i + 1) for i in range(1, size_y - 1, 2)]
    middle += [(b, a) for a, b in middle]
    got_middle = lax.ppermute(jnp.where(odd_y, high, low), gy, middle)
    got_pair = lax.ppermute(jnp.where(odd_y, low, high), gy, [(i, i ^ 1) for i in range(size_y)])
    right = jnp.where(odd_y, got_middle, got_pair)
    left = jnp.where(odd_y, got_pair, got_middle)
    down, up = call(rows_kernel, [shape(FIELDS + 2, 4, 128)] * 2, 2)(fields, right, left)
    odd = lax.axis_index(gx) % 2 == 1
    outer = [(i, i + 1) for i in range(1, size_x - 1, 2)]
    outer += [(b, a) for a, b in outer]
    got_outer = lax.ppermute(jnp.where(odd, up, down), gx, outer)
    got_inner = lax.ppermute(jnp.where(odd, down, up), gx, [(i, i ^ 1) for i in range(size_x)])
    following = jnp.where(odd, got_outer, got_inner)
    previous = jnp.where(odd, got_inner, got_outer)
    vectors, row = call(
        krylov_kernel,
        [shape(4, 2, LEVELS, 8, 128), shape(1, 128)],
        8,
        VMEM((4, 2, LEVELS, 16, 256), F32),
        VMEM((LEVELS, 16, 256), F32),
        VMEM((len(FACTORS), LEVELS - 1, 16, 256), F32),
        VMEM((2, LEVELS, 16, 256), F32),
        VMEM((2, LEVELS, 16, 256), F32),
        VMEM((2, LEVELS, 16, 256), F32),
        VMEM((16, 256), F32),
        VMEM((16, 256), F32),
    )(fields, left, right, following, previous)
    row = jnp.sum(everywhere(row, "near"), axis=0)
    rows = everywhere(row, ("far", "gy"))[:, 0]
    return call(combine_kernel, [shape(2, LEVELS, 8, 128)] * 2, 4)(vectors, rows)


def solution(mesh):
    size_x, size_y = mesh.devices.shape
    split = Mesh(mesh.devices.reshape(8, size_x // 8, size_y), ("far", "near", "gy"))
    gx = ("far", "near")
    vector, plane = P(None, None, gx, "gy"), P(gx, "gy")
    return jax.shard_map(
        local,
        mesh=split,
        in_specs=(vector, P(None, gx, "gy"), plane, plane),
        out_specs=(vector, vector),
        check_vma=False,
    )
```

```python
import jax
import jax.numpy as jnp
from jax import lax
from jax.experimental import pallas as pl
from jax.experimental.pallas import tpu as pltpu
from jax.sharding import Mesh, PartitionSpec as P

LEVELS = 11
FIELDS = 3 * LEVELS + 2
SCALE = 16.0
SHIFTS = (8.0, 2.0, 20.0)
FACTORS = (1.0, 2.0, 4.0, 1.0 / 3.0, 2.0 / 3.0, 5.0 / 3.0)
F32 = jnp.float32
VMEM = pltpu.VMEM


def side_kernel(src_ref, eta_ref, fric_ref, mask_ref, fields_ref, low_ref, high_ref, mask, sems):
    parts = [
        (src_ref.at[0], fields_ref.at[0:LEVELS]),
        (src_ref.at[1], fields_ref.at[LEVELS : 2 * LEVELS]),
        (eta_ref, fields_ref.at[2 * LEVELS : 3 * LEVELS]),
        (fric_ref, fields_ref.at[3 * LEVELS]),
        (mask_ref, mask),
    ]
    copies = [pltpu.make_async_copy(a, b, sems.at[n]) for n, (a, b) in enumerate(parts)]
    for copy in copies:
        copy.start()
    for copy in copies:
        copy.wait()
    fields_ref[FIELDS - 1] = mask[...].astype(F32)
    lane = lax.broadcasted_iota(jnp.int32, (8, 128), 1)
    low = jnp.zeros((8, 128), F32)
    high = jnp.zeros((8, 128), F32)
    for f in range(FIELDS):
        value = fields_ref[f]
        place = (lane >= 3 * f) & (lane < 3 * f + 3)
        low = jnp.where(place, pltpu.roll(value, 3 * f, 1) if f else value, low)
        high = jnp.where(place, pltpu.roll(value, (3 * f - 125) % 128, 1), high)
    low_ref[...] = low
    high_ref[...] = high


def rows_kernel(fields_ref, right_ref, left_ref, down_ref, up_ref):
    for f in range(FIELDS):
        value = fields_ref[f]
        down_ref[f] = value[0:4]
        up_ref[f] = value[4:8]
    for f, value in ((FIELDS, right_ref[...]), (FIELDS + 1, left_ref[...])):
        down_ref[f] = value[0:4]
        up_ref[f] = value[4:8]


def ahead(value, axis):
    return pltpu.roll(value, value.shape[axis] - 1, axis)


def behind(value, axis):
    return pltpu.roll(value, 1, axis)


def flat_modes(plane, after):
    s, d = plane + after, after - plane
    s1, d1 = ahead(s, 0), ahead(d, 0)
    return {"ss": s + s1, "ds": s1 - s, "sd": d + d1, "dd": d1 - d}


def flat_back(modes):
    s = modes["ss"] - modes["ds"] + behind(modes["ss"] + modes["ds"], 0)
    d = modes["sd"] - modes["dd"] + behind(modes["sd"] + modes["dd"], 0)
    return s - d, s + d


def layer(lower, upper, eta):
    whole, double, four, third, two_thirds, five_thirds = eta
    modes = []
    for c in (0, 1):
        m = {}
        for xy in ("ss", "ds", "sd", "dd"):
            m[xy + "d"] = upper[c][xy] - lower[c][xy]
            if xy != "ss":
                m[xy + "s"] = upper[c][xy] + lower[c][xy]
        modes.append(m)
    low, high = [], []
    for c in (0, 1):
        u, v = modes[c], modes[1 - c]
        first, second = ("ds", "sd") if c == 0 else ("sd", "ds")
        up = {
            first + "s": double * (u[first + "s"] + u[first + "s"] + v[second + "s"]),
            second + "s": whole * (u[second + "s"] + v[first + "s"]),
            first + "d": two_thirds * (4.0 * u[first + "d"] + v[second + "d"]),
            second + "d": third * (5.0 * u[second + "d"] + v[first + "d"]),
            "dds": five_thirds * u["dds"],
            "ddd": whole * u["ddd"],
        }
        ssd = four * u["ssd"]
        lo, hi = {"ss": -ssd}, {"ss": ssd}
        for xy in ("ds", "sd", "dd"):
            lo[xy] = up[xy + "s"] - up[xy + "d"]
            hi[xy] = up[xy + "s"] + up[xy + "d"]
        low.append(lo)
        high.append(hi)
    return low, high


def krylov_kernel(
    fields_ref, left_ref, right_ref, next_ref, prev_ref,
    out_ref, row_ref, vec, eta, cell, after, near, far, frict, mask,
):
    lane = lax.broadcasted_iota(jnp.int32, (16, 128), 1)
    left = jnp.concatenate([left_ref[...], next_ref[FIELDS + 1], prev_ref[FIELDS + 1]], 0)
    right = jnp.concatenate([right_ref[...], next_ref[FIELDS], prev_ref[FIELDS]], 0)
    def plane(f):
        own = jnp.concatenate([fields_ref[f], next_ref[f], prev_ref[f]], 0)
        from_left = pltpu.roll(left, (125 - 3 * f) % 128, 1)
        from_right = pltpu.roll(right, (-3 * f) % 128, 1) if f else right
        zero = jnp.zeros((16, 128), F32)
        side = jnp.where(lane >= 125, from_left, jnp.where(lane < 3, from_right, zero))
        return jnp.concatenate([own, side], 1)

    for l in range(LEVELS):
        eta[l] = plane(2 * LEVELS + l)
    mask[...] = plane(3 * LEVELS + 1)
    frict[...] = plane(3 * LEVELS) * (1.0 / SCALE)
    for l in range(LEVELS):
        vec[0, 0, l] = plane(l)
        vec[0, 1, l] = plane(LEVELS + l)
    for l in range(LEVELS - 1):
        value = (eta[l] + eta[l + 1]) * (0.125 / SCALE / 16.0)
        cell[0, l] = value + ahead(value, 1)
    for l in range(LEVELS - 1):
        value = cell[0, l] + ahead(cell[0, l], 0)
        for n, factor in enumerate(FACTORS):
            cell[n, l] = factor * value
    for l in range(LEVELS):
        for c in (0, 1):
            vec[0, c, l] = vec[0, c, l] * mask[...]

    for k in range(3):
        shift = SHIFTS[k] / SCALE

        for c in (0, 1):
            for l in range(LEVELS):
                after[c, l] = ahead(vec[k, c, l], 1)
        for side in (slice(0, 128), slice(128, 256)):
            lower, pending = None, None
            for l in range(LEVELS):
                upper = [
                    flat_modes(vec[k, c, l, :, side], after[c, l, :, side]) for c in (0, 1)
                ]
                if l:
                    eta_parts = [cell[n, l - 1, :, side] for n in range(len(FACTORS))]
                    sums, high = layer(lower, upper, eta_parts)
                    if pending is not None:
                        sums = [{m: sums[c][m] + pending[c][m] for m in sums[c]} for c in (0, 1)]
                    for c in (0, 1):
                        near[c, l - 1, :, side], far[c, l - 1, :, side] = flat_back(sums[c])
                    pending = high
                lower = upper
            for c in (0, 1):
                near[c, LEVELS - 1, :, side], far[c, LEVELS - 1, :, side] = flat_back(pending[c])
        for c in (0, 1):
            for l in range(LEVELS):
                if k < 2:
                    image = near[c, l] + behind(far[c, l], 1)
                    value = vec[k, c, l]
                    if l == 0:
                        image = image + frict[...] * value
                    vec[k + 1, c, l] = image * mask[...] - shift * value
                else:
                    image = near[c, l, 0:8, 0:128] + behind(far[c, l, 0:8], 1)[:, 0:128]
                    value = vec[k, c, l, 0:8, 0:128]
                    if l == 0:
                        image = image + frict[0:8, 0:128] * value
                    vec[k + 1, c, l, 0:8, 0:128] = image * mask[0:8, 0:128] - shift * value

    pairs = ((0, 0), (0, 1), (0, 2), (1, 1), (1, 2), (2, 2), (1, 3), (2, 3))
    sums = [jnp.zeros((8, 128), F32) for _ in pairs]
    for c in (0, 1):
        for l in range(LEVELS):
            v = [vec[k, c, l, 0:8, 0:128] for k in range(4)]
            for k in range(4):
                out_ref[k, c, l] = v[k]
            sums = [s + v[i] * v[j] for s, (i, j) in zip(sums, pairs)]
    stacked = jnp.concatenate([jnp.sum(s, axis=0, keepdims=True) for s in sums], 0)
    totals = jnp.sum(stacked, axis=1, keepdims=True)
    ids = [lax.broadcasted_iota(jnp.int32, (8, 128), a) for a in (0, 1)]
    spread = jnp.where(ids[0] == ids[1], totals, 0.0)
    row_ref[...] = jnp.sum(spread, axis=0, keepdims=True)


def coordinates(gram):
    def dot(a, b):
        total = None
        for i in range(len(a)):
            for j in range(len(b)):
                term = a[i] * b[j] * gram[min(i, j), max(i, j)]
                total = term if total is None else total + term
        return total

    def added(a, b, factor):
        size = max(len(a), len(b))
        out = []
        for i in range(size):
            if i >= len(b):
                out.append(a[i])
            elif i >= len(a):
                out.append(factor * b[i])
            else:
                out.append(a[i] + factor * b[i])
        return out

    one = jnp.ones_like(gram[0, 0])
    residual, direction, answer = [one], [one], []
    norm = gram[0, 0]
    for k in range(3):
        image = [SHIFTS[i] * direction[i] for i in range(k + 1)] + [SCALE * direction[k]]
        for i in range(1, k + 1):
            image[i] = image[i] + SCALE * direction[i - 1]
        alpha = norm / dot(direction, image)
        answer = added(answer, direction, alpha)
        residual = added(residual, image, -alpha)
        if k < 2:
            fresh = dot(residual, residual)
            direction = added(residual, direction, fresh / norm)
            norm = fresh
    return answer, residual


def combine_kernel(vec_ref, rows_ref, answer_ref, residual_ref):
    row = jnp.sum(rows_ref[...], axis=0, keepdims=True)
    ids = [lax.broadcasted_iota(jnp.int32, (8, 128), a) for a in (0, 1)]
    totals = jnp.sum(jnp.where(ids[0] == ids[1], row, 0.0), axis=1, keepdims=True)
    tile = jnp.broadcast_to(totals, (8, 128))
    pairs = ((0, 0), (0, 1), (0, 2), (1, 1), (1, 2), (2, 2), (1, 3), (2, 3))
    gram = {pair: tile[n : n + 1] for n, pair in enumerate(pairs)}
    gram[0, 3] = gram[1, 2] + ((SHIFTS[0] - SHIFTS[2]) / SCALE) * gram[0, 2]
    answer, residual = coordinates(gram)
    answer = [jnp.broadcast_to(a, (8, 128)) for a in answer]
    residual = [jnp.broadcast_to(a, (8, 128)) for a in residual]
    for c in (0, 1):
        for l in range(LEVELS):
            v = [vec_ref[k, c, l] for k in range(4)]
            answer_ref[c, l] = answer[0] * v[0] + answer[1] * v[1] + answer[2] * v[2]
            residual_ref[c, l] = (
                residual[0] * v[0] + residual[1] * v[1] + residual[2] * v[2] + residual[3] * v[3]
            )


def call(kernel, outs, megabytes, *scratch, space=VMEM):
    def run(*args):
        return pl.pallas_call(
            kernel,
            out_shape=tuple(outs),
            in_specs=[pl.BlockSpec(memory_space=space)] * len(args),
            out_specs=tuple([pl.BlockSpec(memory_space=VMEM)] * len(outs)),
            scratch_shapes=list(scratch),
            compiler_params=pltpu.CompilerParams(vmem_limit_bytes=megabytes << 20),
        )(*args)

    return run


def shape(*dims):
    return jax.ShapeDtypeStruct(dims, F32)


def everywhere(row, axes):
    size = lax.axis_size(axes)
    spread = jnp.broadcast_to(row[None], (size, 1, 128))
    return lax.all_to_all(spread, axes, 0, 0, tiled=True)


def local(*arguments):
    gx, gy = ("far", "mid", "core"), "gy"
    size_x, size_y = lax.axis_size(gx), lax.axis_size(gy)
    fields, low, high = call(
        side_kernel,
        [shape(FIELDS, 8, 128), shape(8, 128), shape(8, 128)],
        2,
        VMEM((8, 128), jnp.int32),
        pltpu.SemaphoreType.DMA((5,)),
        space=pltpu.HBM,
    )(*[pltpu.with_memory_space_constraint(a, pltpu.HBM) for a in arguments])
    odd_y = lax.axis_index(gy) % 2 == 1
    middle = [(i, i + 1) for i in range(1, size_y - 1, 2)]
    middle += [(b, a) for a, b in middle]
    got_middle = lax.ppermute(jnp.where(odd_y, high, low), gy, middle)
    duos = [[i, i + 1] for i in range(0, size_y, 2)]
    duo = lax.all_gather(jnp.where(odd_y, low, high), gy, axis_index_groups=duos)
    got_pair = jnp.where(odd_y, duo[0], duo[1])
    right = jnp.where(odd_y, got_middle, got_pair)
    left = jnp.where(odd_y, got_pair, got_middle)
    down, up = call(rows_kernel, [shape(FIELDS + 2, 4, 128)] * 2, 2)(fields, right, left)
    odd = lax.axis_index(gx) % 2 == 1
    outer = [(i, i + 1) for i in range(1, size_x - 1, 2)]
    outer += [(b, a) for a, b in outer]
    got_outer = lax.ppermute(jnp.where(odd, up, down), gx, outer)
    both = lax.all_gather(jnp.where(odd, down, up), "core")
    following = jnp.where(odd, got_outer, both[1])
    previous = jnp.where(odd, both[0], got_outer)
    vectors, row = call(
        krylov_kernel,
        [shape(4, 2, LEVELS, 8, 128), shape(1, 128)],
        8,
        VMEM((4, 2, LEVELS, 16, 256), F32),
        VMEM((LEVELS, 16, 256), F32),
        VMEM((len(FACTORS), LEVELS - 1, 16, 256), F32),
        VMEM((2, LEVELS, 16, 256), F32),
        VMEM((2, LEVELS, 16, 256), F32),
        VMEM((2, LEVELS, 16, 256), F32),
        VMEM((16, 256), F32),
        VMEM((16, 256), F32),
    )(fields, left, right, following, previous)
    row = jnp.sum(everywhere(row, ("mid", "core")), axis=0)
    rows = everywhere(row, ("far", "gy"))[:, 0]
    return call(combine_kernel, [shape(2, LEVELS, 8, 128)] * 2, 4)(vectors, rows)


def solution(mesh):
    size_x, size_y = mesh.devices.shape
    split = Mesh(mesh.devices.reshape(8, size_x // 16, 2, size_y), ("far", "mid", "core", "gy"))
    gx = ("far", "mid", "core")
    vector, plane = P(None, None, gx, "gy"), P(gx, "gy")
    return jax.shard_map(
        local,
        mesh=split,
        in_specs=(vector, P(None, gx, "gy"), plane, plane),
        out_specs=(vector, vector),
        check_vma=False,
    )
```

```python
import jax
import jax.numpy as jnp
from jax import lax
from jax.experimental import pallas as pl
from jax.experimental.pallas import tpu as pltpu
from jax.sharding import Mesh, PartitionSpec as P

LEVELS = 11
FIELDS = 3 * LEVELS + 2
SCALE = 16.0
SHIFTS = (8.0, 2.0, 20.0)
FACTORS = (1.0, 2.0, 4.0, 1.0 / 3.0, 2.0 / 3.0, 5.0 / 3.0)
F32 = jnp.float32
VMEM = pltpu.VMEM


def side_kernel(src_ref, eta_ref, fric_ref, mask_ref, fields_ref, low_ref, high_ref, mask, sems):
    parts = [
        (src_ref.at[0], fields_ref.at[0:LEVELS]),
        (src_ref.at[1], fields_ref.at[LEVELS : 2 * LEVELS]),
        (eta_ref, fields_ref.at[2 * LEVELS : 3 * LEVELS]),
        (fric_ref, fields_ref.at[3 * LEVELS]),
        (mask_ref, mask),
    ]
    copies = [pltpu.make_async_copy(a, b, sems.at[n]) for n, (a, b) in enumerate(parts)]
    for copy in copies:
        copy.start()
    for copy in copies:
        copy.wait()
    fields_ref[FIELDS - 1] = mask[...].astype(F32)
    lane = lax.broadcasted_iota(jnp.int32, (8, 128), 1)
    low = jnp.zeros((8, 128), F32)
    high = jnp.zeros((8, 128), F32)
    for f in range(FIELDS):
        value = fields_ref[f]
        place = (lane >= 3 * f) & (lane < 3 * f + 3)
        low = jnp.where(place, pltpu.roll(value, 3 * f, 1) if f else value, low)
        high = jnp.where(place, pltpu.roll(value, (3 * f - 125) % 128, 1), high)
    low_ref[...] = low
    high_ref[...] = high


def rows_kernel(fields_ref, right_ref, left_ref, down_ref, up_ref):
    for f in range(FIELDS):
        value = fields_ref[f]
        down_ref[f] = value[0:4]
        up_ref[f] = value[4:8]
    for f, value in ((FIELDS, right_ref[...]), (FIELDS + 1, left_ref[...])):
        down_ref[f] = value[0:4]
        up_ref[f] = value[4:8]


def ahead(value, axis):
    return pltpu.roll(value, value.shape[axis] - 1, axis)


def behind(value, axis):
    return pltpu.roll(value, 1, axis)


def flat_modes(plane, after):
    s, d = plane + after, after - plane
    s1, d1 = ahead(s, 0), ahead(d, 0)
    return {"ss": s + s1, "ds": s1 - s, "sd": d + d1, "dd": d1 - d}


def flat_back(modes):
    s = modes["ss"] - modes["ds"] + behind(modes["ss"] + modes["ds"], 0)
    d = modes["sd"] - modes["dd"] + behind(modes["sd"] + modes["dd"], 0)
    return s - d, s + d


def layer(lower, upper, eta):
    whole, double, four, third, two_thirds, five_thirds = eta
    modes = []
    for c in (0, 1):
        m = {}
        for xy in ("ss", "ds", "sd", "dd"):
            m[xy + "d"] = upper[c][xy] - lower[c][xy]
            if xy != "ss":
                m[xy + "s"] = upper[c][xy] + lower[c][xy]
        modes.append(m)
    low, high = [], []
    for c in (0, 1):
        u, v = modes[c], modes[1 - c]
        first, second = ("ds", "sd") if c == 0 else ("sd", "ds")
        up = {
            first + "s": double * (u[first + "s"] + u[first + "s"] + v[second + "s"]),
            second + "s": whole * (u[second + "s"] + v[first + "s"]),
            first + "d": two_thirds * (4.0 * u[first + "d"] + v[second + "d"]),
            second + "d": third * (5.0 * u[second + "d"] + v[first + "d"]),
            "dds": five_thirds * u["dds"],
            "ddd": whole * u["ddd"],
        }
        ssd = four * u["ssd"]
        lo, hi = {"ss": -ssd}, {"ss": ssd}
        for xy in ("ds", "sd", "dd"):
            lo[xy] = up[xy + "s"] - up[xy + "d"]
            hi[xy] = up[xy + "s"] + up[xy + "d"]
        low.append(lo)
        high.append(hi)
    return low, high


def krylov_kernel(
    fields_ref, left_ref, right_ref, next_ref, prev_ref,
    out_ref, row_ref, vec, eta, cell, after, near, far, frict, mask,
):
    lane = lax.broadcasted_iota(jnp.int32, (16, 128), 1)
    left = jnp.concatenate([left_ref[...], next_ref[FIELDS + 1], prev_ref[FIELDS + 1]], 0)
    right = jnp.concatenate([right_ref[...], next_ref[FIELDS], prev_ref[FIELDS]], 0)
    def plane(f):
        own = jnp.concatenate([fields_ref[f], next_ref[f], prev_ref[f]], 0)
        from_left = pltpu.roll(left, (125 - 3 * f) % 128, 1)
        from_right = pltpu.roll(right, (-3 * f) % 128, 1) if f else right
        zero = jnp.zeros((16, 128), F32)
        side = jnp.where(lane >= 125, from_left, jnp.where(lane < 3, from_right, zero))
        return jnp.concatenate([own, side], 1)

    for l in range(LEVELS):
        eta[l] = plane(2 * LEVELS + l)
    mask[...] = plane(3 * LEVELS + 1)
    frict[...] = plane(3 * LEVELS) * (1.0 / SCALE)
    for l in range(LEVELS):
        vec[0, 0, l] = plane(l)
        vec[0, 1, l] = plane(LEVELS + l)
    for l in range(LEVELS - 1):
        value = (eta[l] + eta[l + 1]) * (0.125 / SCALE / 16.0)
        cell[0, l] = value + ahead(value, 1)
    for l in range(LEVELS - 1):
        value = cell[0, l] + ahead(cell[0, l], 0)
        for n, factor in enumerate(FACTORS):
            cell[n, l] = factor * value
    for l in range(LEVELS):
        for c in (0, 1):
            vec[0, c, l] = vec[0, c, l] * mask[...]

    for k in range(3):
        shift = SHIFTS[k] / SCALE

        for c in (0, 1):
            for l in range(LEVELS):
                after[c, l] = ahead(vec[k, c, l], 1)
        for side in (slice(0, 128), slice(128, 256)):
            lower, pending = None, None
            for l in range(LEVELS):
                upper = [
                    flat_modes(vec[k, c, l, :, side], after[c, l, :, side]) for c in (0, 1)
                ]
                if l:
                    eta_parts = [cell[n, l - 1, :, side] for n in range(len(FACTORS))]
                    sums, high = layer(lower, upper, eta_parts)
                    if pending is not None:
                        sums = [{m: sums[c][m] + pending[c][m] for m in sums[c]} for c in (0, 1)]
                    for c in (0, 1):
                        near[c, l - 1, :, side], far[c, l - 1, :, side] = flat_back(sums[c])
                    pending = high
                lower = upper
            for c in (0, 1):
                near[c, LEVELS - 1, :, side], far[c, LEVELS - 1, :, side] = flat_back(pending[c])
        for c in (0, 1):
            for l in range(LEVELS):
                if k < 2:
                    image = near[c, l] + behind(far[c, l], 1)
                    value = vec[k, c, l]
                    if l == 0:
                        image = image + frict[...] * value
                    vec[k + 1, c, l] = image * mask[...] - shift * value
                else:
                    image = near[c, l, 0:8, 0:128] + behind(far[c, l, 0:8], 1)[:, 0:128]
                    value = vec[k, c, l, 0:8, 0:128]
                    if l == 0:
                        image = image + frict[0:8, 0:128] * value
                    vec[k + 1, c, l, 0:8, 0:128] = image * mask[0:8, 0:128] - shift * value

    pairs = ((0, 0), (0, 1), (0, 2), (1, 1), (1, 2), (2, 2), (1, 3), (2, 3))
    sums = [jnp.zeros((8, 128), F32) for _ in pairs]
    for c in (0, 1):
        for l in range(LEVELS):
            v = [vec[k, c, l, 0:8, 0:128] for k in range(4)]
            for k in range(4):
                out_ref[k, c, l] = v[k]
            sums = [s + v[i] * v[j] for s, (i, j) in zip(sums, pairs)]
    stacked = jnp.concatenate([jnp.sum(s, axis=0, keepdims=True) for s in sums], 0)
    totals = jnp.sum(stacked, axis=1, keepdims=True)
    ids = [lax.broadcasted_iota(jnp.int32, (8, 128), a) for a in (0, 1)]
    spread = jnp.where(ids[0] == ids[1], totals, 0.0)
    row_ref[...] = jnp.broadcast_to(jnp.sum(spread, axis=0, keepdims=True), (8, 128))


def coordinates(gram):
    def dot(a, b):
        total = None
        for i in range(len(a)):
            for j in range(len(b)):
                term = a[i] * b[j] * gram[min(i, j), max(i, j)]
                total = term if total is None else total + term
        return total

    def added(a, b, factor):
        size = max(len(a), len(b))
        out = []
        for i in range(size):
            if i >= len(b):
                out.append(a[i])
            elif i >= len(a):
                out.append(factor * b[i])
            else:
                out.append(a[i] + factor * b[i])
        return out

    one = jnp.ones_like(gram[0, 0])
    residual, direction, answer = [one], [one], []
    norm = gram[0, 0]
    for k in range(3):
        image = [SHIFTS[i] * direction[i] for i in range(k + 1)] + [SCALE * direction[k]]
        for i in range(1, k + 1):
            image[i] = image[i] + SCALE * direction[i - 1]
        alpha = norm / dot(direction, image)
        answer = added(answer, direction, alpha)
        residual = added(residual, image, -alpha)
        if k < 2:
            fresh = dot(residual, residual)
            direction = added(residual, direction, fresh / norm)
            norm = fresh
    return answer, residual


def combine_kernel(vec_ref, rows_ref, answer_ref, residual_ref):
    row = jnp.sum(rows_ref[...], axis=0, keepdims=True)
    ids = [lax.broadcasted_iota(jnp.int32, (8, 128), a) for a in (0, 1)]
    totals = jnp.sum(jnp.where(ids[0] == ids[1], row, 0.0), axis=1, keepdims=True)
    tile = jnp.broadcast_to(totals, (8, 128))
    pairs = ((0, 0), (0, 1), (0, 2), (1, 1), (1, 2), (2, 2), (1, 3), (2, 3))
    gram = {pair: tile[n : n + 1] for n, pair in enumerate(pairs)}
    gram[0, 3] = gram[1, 2] + ((SHIFTS[0] - SHIFTS[2]) / SCALE) * gram[0, 2]
    answer, residual = coordinates(gram)
    answer = [jnp.broadcast_to(a, (8, 128)) for a in answer]
    residual = [jnp.broadcast_to(a, (8, 128)) for a in residual]
    for c in (0, 1):
        for l in range(LEVELS):
            v = [vec_ref[k, c, l] for k in range(4)]
            answer_ref[c, l] = answer[0] * v[0] + answer[1] * v[1] + answer[2] * v[2]
            residual_ref[c, l] = (
                residual[0] * v[0] + residual[1] * v[1] + residual[2] * v[2] + residual[3] * v[3]
            )


def call(kernel, outs, megabytes, *scratch, space=VMEM):
    def run(*args):
        return pl.pallas_call(
            kernel,
            out_shape=tuple(outs),
            in_specs=[pl.BlockSpec(memory_space=space)] * len(args),
            out_specs=tuple([pl.BlockSpec(memory_space=VMEM)] * len(outs)),
            scratch_shapes=list(scratch),
            compiler_params=pltpu.CompilerParams(vmem_limit_bytes=megabytes << 20),
        )(*args)

    return run


def shape(*dims):
    return jax.ShapeDtypeStruct(dims, F32)


def everywhere(row, axes):
    size = lax.axis_size(axes)
    spread = jnp.broadcast_to(row[None], (size, 1, 128))
    return lax.all_to_all(spread, axes, 0, 0, tiled=True)


def local(*arguments):
    gx, gy = ("far", "mid", "core"), "gy"
    size_x, size_y = lax.axis_size(gx), lax.axis_size(gy)
    fields, low, high = call(
        side_kernel,
        [shape(FIELDS, 8, 128), shape(8, 128), shape(8, 128)],
        2,
        VMEM((8, 128), jnp.int32),
        pltpu.SemaphoreType.DMA((5,)),
        space=pltpu.HBM,
    )(*[pltpu.with_memory_space_constraint(a, pltpu.HBM) for a in arguments])
    odd_y = lax.axis_index(gy) % 2 == 1
    middle = [(i, i + 1) for i in range(1, size_y - 1, 2)]
    middle += [(b, a) for a, b in middle]
    got_middle = lax.ppermute(jnp.where(odd_y, high, low), gy, middle)
    duos = [[i, i + 1] for i in range(0, size_y, 2)]
    duo = lax.all_gather(jnp.where(odd_y, low, high), gy, axis_index_groups=duos)
    got_pair = jnp.where(odd_y, duo[0], duo[1])
    right = jnp.where(odd_y, got_middle, got_pair)
    left = jnp.where(odd_y, got_pair, got_middle)
    down, up = call(rows_kernel, [shape(FIELDS + 3, 4, 128)] * 2, 2)(fields, right, left)
    odd = lax.axis_index(gx) % 2 == 1
    outer = [(i, i + 1) for i in range(1, size_x - 1, 2)]
    outer += [(b, a) for a, b in outer]
    got_outer = lax.ppermute(jnp.where(odd, up, down), gx, outer)
    both = lax.all_gather(jnp.where(odd, down, up), "core")
    following = jnp.where(odd, got_outer, both[1])
    previous = jnp.where(odd, both[0], got_outer)
    vectors, row = call(
        krylov_kernel,
        [shape(4, 2, LEVELS, 8, 128), shape(8, 128)],
        8,
        VMEM((4, 2, LEVELS, 16, 256), F32),
        VMEM((LEVELS, 16, 256), F32),
        VMEM((len(FACTORS), LEVELS - 1, 16, 256), F32),
        VMEM((2, LEVELS, 16, 256), F32),
        VMEM((2, LEVELS, 16, 256), F32),
        VMEM((2, LEVELS, 16, 256), F32),
        VMEM((16, 256), F32),
        VMEM((16, 256), F32),
    )(fields, left, right, following, previous)
    row = jnp.sum(everywhere(row[0:1], ("mid", "core")), axis=0)
    rows = everywhere(row, ("far", "gy"))[:, 0]
    return call(combine_kernel, [shape(2, LEVELS, 8, 128)] * 2, 4)(vectors, rows)


def solution(mesh):
    size_x, size_y = mesh.devices.shape
    split = Mesh(mesh.devices.reshape(8, size_x // 16, 2, size_y), ("far", "mid", "core", "gy"))
    gx = ("far", "mid", "core")
    vector, plane = P(None, None, gx, "gy"), P(gx, "gy")
    return jax.shard_map(
        local,
        mesh=split,
        in_specs=(vector, P(None, gx, "gy"), plane, plane),
        out_specs=(vector, vector),
        check_vma=False,
    )
```

```python
import jax
import jax.numpy as jnp
from jax import lax
from jax.experimental import pallas as pl
from jax.experimental.pallas import tpu as pltpu
from jax.sharding import Mesh, PartitionSpec as P

LEVELS = 11
FIELDS = 3 * LEVELS + 2
SCALE = 16.0
SHIFTS = (8.0, 2.0, 20.0)
FACTORS = (1.0, 2.0, 4.0, 1.0 / 3.0, 2.0 / 3.0, 5.0 / 3.0)
F32 = jnp.float32
VMEM = pltpu.VMEM


def side_kernel(
    src_ref, eta_ref, fric_ref, mask_ref, odd_y_ref, fields_ref, middle_ref, pair_ref, mask, sems
):
    parts = [
        (src_ref.at[0], fields_ref.at[0:LEVELS]),
        (src_ref.at[1], fields_ref.at[LEVELS : 2 * LEVELS]),
        (eta_ref, fields_ref.at[2 * LEVELS : 3 * LEVELS]),
        (fric_ref, fields_ref.at[3 * LEVELS]),
        (mask_ref, mask),
    ]
    copies = [pltpu.make_async_copy(a, b, sems.at[n]) for n, (a, b) in enumerate(parts)]
    for copy in copies:
        copy.start()
    for copy in copies:
        copy.wait()
    fields_ref[FIELDS - 1] = mask[...].astype(F32)
    lane = lax.broadcasted_iota(jnp.int32, (8, 128), 1)
    low = jnp.zeros((8, 128), F32)
    high = jnp.zeros((8, 128), F32)
    for f in range(FIELDS):
        value = fields_ref[f]
        place = (lane >= 3 * f) & (lane < 3 * f + 3)
        low = jnp.where(place, pltpu.roll(value, 3 * f, 1) if f else value, low)
        high = jnp.where(place, pltpu.roll(value, (3 * f - 125) % 128, 1), high)
    odd_y = odd_y_ref[...] > 0
    middle_ref[...] = jnp.where(odd_y, high, low)
    pair_ref[...] = jnp.where(odd_y, low, high)


def rows_kernel(
    fields_ref, middle_ref, duo_ref, odd_y_ref, odd_ref, outer_ref, inner_ref, left_ref, right_ref
):
    odd_y = odd_y_ref[...] > 0
    pair = jnp.where(odd_y, duo_ref[0], duo_ref[1])
    right = jnp.where(odd_y, middle_ref[...], pair)
    left = jnp.where(odd_y, pair, middle_ref[...])
    left_ref[...] = left
    right_ref[...] = right
    odd = odd_ref[0:4] > 0
    for f in range(FIELDS + 2):
        value = fields_ref[f] if f < FIELDS else (right, left)[f - FIELDS]
        outer_ref[f] = jnp.where(odd, value[4:8], value[0:4])
        inner_ref[f] = jnp.where(odd, value[0:4], value[4:8])


def ahead(value, axis):
    return pltpu.roll(value, value.shape[axis] - 1, axis)


def behind(value, axis):
    return pltpu.roll(value, 1, axis)


def flat_modes(plane, after):
    s, d = plane + after, after - plane
    s1, d1 = ahead(s, 0), ahead(d, 0)
    return {"ss": s + s1, "ds": s1 - s, "sd": d + d1, "dd": d1 - d}


def flat_back(modes):
    s = modes["ss"] - modes["ds"] + behind(modes["ss"] + modes["ds"], 0)
    d = modes["sd"] - modes["dd"] + behind(modes["sd"] + modes["dd"], 0)
    return s - d, s + d


def layer(lower, upper, eta):
    whole, double, four, third, two_thirds, five_thirds = eta
    modes = []
    for c in (0, 1):
        m = {}
        for xy in ("ss", "ds", "sd", "dd"):
            m[xy + "d"] = upper[c][xy] - lower[c][xy]
            if xy != "ss":
                m[xy + "s"] = upper[c][xy] + lower[c][xy]
        modes.append(m)
    low, high = [], []
    for c in (0, 1):
        u, v = modes[c], modes[1 - c]
        first, second = ("ds", "sd") if c == 0 else ("sd", "ds")
        up = {
            first + "s": double * (u[first + "s"] + u[first + "s"] + v[second + "s"]),
            second + "s": whole * (u[second + "s"] + v[first + "s"]),
            first + "d": two_thirds * (4.0 * u[first + "d"] + v[second + "d"]),
            second + "d": third * (5.0 * u[second + "d"] + v[first + "d"]),
            "dds": five_thirds * u["dds"],
            "ddd": whole * u["ddd"],
        }
        ssd = four * u["ssd"]
        lo, hi = {"ss": -ssd}, {"ss": ssd}
        for xy in ("ds", "sd", "dd"):
            lo[xy] = up[xy + "s"] - up[xy + "d"]
            hi[xy] = up[xy + "s"] + up[xy + "d"]
        low.append(lo)
        high.append(hi)
    return low, high


def krylov_kernel(
    fields_ref, left_ref, right_ref, outer_ref, both_ref, odd_ref,
    out_ref, row_ref, vec, eta, cell, after, near, far, frict, mask,
):
    lane = lax.broadcasted_iota(jnp.int32, (16, 128), 1)
    odd = odd_ref[0:4] > 0

    def joined(own, f):
        outside = outer_ref[f]
        following = jnp.where(odd, outside, both_ref[1, f])
        previous = jnp.where(odd, both_ref[0, f], outside)
        return jnp.concatenate([own, following, previous], 0)

    left = joined(left_ref[...], FIELDS + 1)
    right = joined(right_ref[...], FIELDS)

    def plane(f):
        own = joined(fields_ref[f], f)
        from_left = pltpu.roll(left, (125 - 3 * f) % 128, 1)
        from_right = pltpu.roll(right, (-3 * f) % 128, 1) if f else right
        zero = jnp.zeros((16, 128), F32)
        side = jnp.where(lane >= 125, from_left, jnp.where(lane < 3, from_right, zero))
        return jnp.concatenate([own, side], 1)

    for l in range(LEVELS):
        eta[l] = plane(2 * LEVELS + l)
    mask[...] = plane(3 * LEVELS + 1)
    frict[...] = plane(3 * LEVELS) * (1.0 / SCALE)
    for l in range(LEVELS):
        vec[0, 0, l] = plane(l)
        vec[0, 1, l] = plane(LEVELS + l)
    for l in range(LEVELS - 1):
        value = (eta[l] + eta[l + 1]) * (0.125 / SCALE / 16.0)
        cell[0, l] = value + ahead(value, 1)
    for l in range(LEVELS - 1):
        value = cell[0, l] + ahead(cell[0, l], 0)
        for n, factor in enumerate(FACTORS):
            cell[n, l] = factor * value
    for l in range(LEVELS):
        for c in (0, 1):
            vec[0, c, l] = vec[0, c, l] * mask[...]

    for k in range(3):
        shift = SHIFTS[k] / SCALE

        for c in (0, 1):
            for l in range(LEVELS):
                after[c, l] = ahead(vec[k, c, l], 1)
        for side in (slice(0, 128), slice(128, 256)):
            lower, pending = None, None
            for l in range(LEVELS):
                upper = [
                    flat_modes(vec[k, c, l, :, side], after[c, l, :, side]) for c in (0, 1)
                ]
                if l:
                    eta_parts = [cell[n, l - 1, :, side] for n in range(len(FACTORS))]
                    sums, high = layer(lower, upper, eta_parts)
                    if pending is not None:
                        sums = [{m: sums[c][m] + pending[c][m] for m in sums[c]} for c in (0, 1)]
                    for c in (0, 1):
                        near[c, l - 1, :, side], far[c, l - 1, :, side] = flat_back(sums[c])
                    pending = high
                lower = upper
            for c in (0, 1):
                near[c, LEVELS - 1, :, side], far[c, LEVELS - 1, :, side] = flat_back(pending[c])
        for c in (0, 1):
            for l in range(LEVELS):
                if k < 2:
                    image = near[c, l] + behind(far[c, l], 1)
                    value = vec[k, c, l]
                    if l == 0:
                        image = image + frict[...] * value
                    vec[k + 1, c, l] = image * mask[...] - shift * value
                else:
                    image = near[c, l, 0:8, 0:128] + behind(far[c, l, 0:8], 1)[:, 0:128]
                    value = vec[k, c, l, 0:8, 0:128]
                    if l == 0:
                        image = image + frict[0:8, 0:128] * value
                    vec[k + 1, c, l, 0:8, 0:128] = image * mask[0:8, 0:128] - shift * value

    pairs = ((0, 0), (0, 1), (0, 2), (1, 1), (1, 2), (2, 2), (1, 3), (2, 3))
    sums = [jnp.zeros((8, 128), F32) for _ in pairs]
    for c in (0, 1):
        for l in range(LEVELS):
            v = [vec[k, c, l, 0:8, 0:128] for k in range(4)]
            for k in range(4):
                out_ref[k, c, l] = v[k]
            sums = [s + v[i] * v[j] for s, (i, j) in zip(sums, pairs)]
    stacked = jnp.concatenate([jnp.sum(s, axis=0, keepdims=True) for s in sums], 0)
    totals = jnp.sum(stacked, axis=1, keepdims=True)
    ids = [lax.broadcasted_iota(jnp.int32, (8, 128), a) for a in (0, 1)]
    spread = jnp.where(ids[0] == ids[1], totals, 0.0)
    row_ref[...] = jnp.broadcast_to(jnp.sum(spread, axis=0, keepdims=True), (8, 128))


def coordinates(gram):
    def dot(a, b):
        total = None
        for i in range(len(a)):
            for j in range(len(b)):
                term = a[i] * b[j] * gram[min(i, j), max(i, j)]
                total = term if total is None else total + term
        return total

    def added(a, b, factor):
        size = max(len(a), len(b))
        out = []
        for i in range(size):
            if i >= len(b):
                out.append(a[i])
            elif i >= len(a):
                out.append(factor * b[i])
            else:
                out.append(a[i] + factor * b[i])
        return out

    one = jnp.ones_like(gram[0, 0])
    residual, direction, answer = [one], [one], []
    norm = gram[0, 0]
    for k in range(3):
        image = [SHIFTS[i] * direction[i] for i in range(k + 1)] + [SCALE * direction[k]]
        for i in range(1, k + 1):
            image[i] = image[i] + SCALE * direction[i - 1]
        alpha = norm / dot(direction, image)
        answer = added(answer, direction, alpha)
        residual = added(residual, image, -alpha)
        if k < 2:
            fresh = dot(residual, residual)
            direction = added(residual, direction, fresh / norm)
            norm = fresh
    return answer, residual


def combine_kernel(vec_ref, rows_ref, answer_ref, residual_ref):
    row = jnp.sum(rows_ref[...], axis=0, keepdims=True)
    ids = [lax.broadcasted_iota(jnp.int32, (8, 128), a) for a in (0, 1)]
    totals = jnp.sum(jnp.where(ids[0] == ids[1], row, 0.0), axis=1, keepdims=True)
    tile = jnp.broadcast_to(totals, (8, 128))
    pairs = ((0, 0), (0, 1), (0, 2), (1, 1), (1, 2), (2, 2), (1, 3), (2, 3))
    gram = {pair: tile[n : n + 1] for n, pair in enumerate(pairs)}
    gram[0, 3] = gram[1, 2] + ((SHIFTS[0] - SHIFTS[2]) / SCALE) * gram[0, 2]
    answer, residual = coordinates(gram)
    answer = [jnp.broadcast_to(a, (8, 128)) for a in answer]
    residual = [jnp.broadcast_to(a, (8, 128)) for a in residual]
    for c in (0, 1):
        for l in range(LEVELS):
            v = [vec_ref[k, c, l] for k in range(4)]
            answer_ref[c, l] = answer[0] * v[0] + answer[1] * v[1] + answer[2] * v[2]
            residual_ref[c, l] = (
                residual[0] * v[0] + residual[1] * v[1] + residual[2] * v[2] + residual[3] * v[3]
            )


def call(kernel, outs, megabytes, *scratch, spaces=()):
    def run(*args):
        return pl.pallas_call(
            kernel,
            out_shape=tuple(outs),
            in_specs=[
                pl.BlockSpec(memory_space=spaces[n] if n < len(spaces) else VMEM)
                for n in range(len(args))
            ],
            out_specs=tuple([pl.BlockSpec(memory_space=VMEM)] * len(outs)),
            scratch_shapes=list(scratch),
            compiler_params=pltpu.CompilerParams(vmem_limit_bytes=megabytes << 20),
        )(*args)

    return run


def shape(*dims):
    return jax.ShapeDtypeStruct(dims, F32)


def everywhere(row, axes):
    size = lax.axis_size(axes)
    spread = jnp.broadcast_to(row[None], (size, 1, 128))
    return lax.all_to_all(spread, axes, 0, 0, tiled=True)


def local(*arguments):
    gx, gy = ("far", "mid", "core"), "gy"
    size_x, size_y = lax.axis_size(gx), lax.axis_size(gy)
    odd_y = jnp.full((8, 128), lax.axis_index(gy) % 2, jnp.int32)
    odd = jnp.full((8, 128), lax.axis_index("core"), jnp.int32)
    fields, to_middle, to_pair = call(
        side_kernel,
        [shape(FIELDS, 8, 128), shape(8, 128), shape(8, 128)],
        2,
        VMEM((8, 128), jnp.int32),
        pltpu.SemaphoreType.DMA((5,)),
        spaces=[pltpu.HBM] * 4,
    )(*[pltpu.with_memory_space_constraint(a, pltpu.HBM) for a in arguments], odd_y)
    middle = [(i, i + 1) for i in range(1, size_y - 1, 2)]
    middle += [(b, a) for a, b in middle]
    got_middle = lax.ppermute(to_middle, gy, middle)
    duos = [[i, i + 1] for i in range(0, size_y, 2)]
    duo = lax.all_gather(to_pair, gy, axis_index_groups=duos)
    to_outer, to_inner, left, right = call(
        rows_kernel, [shape(FIELDS + 3, 4, 128)] * 2 + [shape(8, 128)] * 2, 2
    )(fields, got_middle, duo, odd_y, odd)
    outer = [(i, i + 1) for i in range(1, size_x - 1, 2)]
    outer += [(b, a) for a, b in outer]
    got_outer = lax.ppermute(to_outer, gx, outer)
    both = lax.all_gather(to_inner, "core")
    vectors, row = call(
        krylov_kernel,
        [shape(4, 2, LEVELS, 8, 128), shape(8, 128)],
        8,
        VMEM((4, 2, LEVELS, 16, 256), F32),
        VMEM((LEVELS, 16, 256), F32),
        VMEM((len(FACTORS), LEVELS - 1, 16, 256), F32),
        VMEM((2, LEVELS, 16, 256), F32),
        VMEM((2, LEVELS, 16, 256), F32),
        VMEM((2, LEVELS, 16, 256), F32),
        VMEM((16, 256), F32),
        VMEM((16, 256), F32),
    )(fields, left, right, got_outer, both, odd)
    row = jnp.sum(everywhere(row[0:1], ("mid", "core")), axis=0)
    rows = everywhere(row, ("far", "gy"))[:, 0]
    return call(combine_kernel, [shape(2, LEVELS, 8, 128)] * 2, 4)(vectors, rows)


def solution(mesh):
    size_x, size_y = mesh.devices.shape
    split = Mesh(mesh.devices.reshape(8, size_x // 16, 2, size_y), ("far", "mid", "core", "gy"))
    gx = ("far", "mid", "core")
    vector, plane = P(None, None, gx, "gy"), P(gx, "gy")
    return jax.shard_map(
        local,
        mesh=split,
        in_specs=(vector, P(None, gx, "gy"), plane, plane),
        out_specs=(vector, vector),
        check_vma=False,
    )
```

```python
import jax
import jax.numpy as jnp
from jax import lax
from jax.experimental import pallas as pl
from jax.experimental.pallas import tpu as pltpu
from jax.sharding import Mesh, PartitionSpec as P

LEVELS = 11
FIELDS = 3 * LEVELS + 2
SCALE = 16.0
SHIFTS = (8.0, 2.0, 20.0)
FACTORS = (1.0, 2.0, 4.0, 1.0 / 3.0, 2.0 / 3.0, 5.0 / 3.0)
F32 = jnp.float32
VMEM = pltpu.VMEM


def side_kernel(
    src_ref, eta_ref, fric_ref, mask_ref, odd_y_ref, fields_ref, middle_ref, pair_ref, mask, sems
):
    parts = [
        (src_ref.at[0], fields_ref.at[0:LEVELS]),
        (src_ref.at[1], fields_ref.at[LEVELS : 2 * LEVELS]),
        (eta_ref, fields_ref.at[2 * LEVELS : 3 * LEVELS]),
        (fric_ref, fields_ref.at[3 * LEVELS]),
        (mask_ref, mask),
    ]
    copies = [pltpu.make_async_copy(a, b, sems.at[n]) for n, (a, b) in enumerate(parts)]
    for copy in copies:
        copy.start()
    for copy in copies:
        copy.wait()
    fields_ref[FIELDS - 1] = mask[...].astype(F32)
    lane = lax.broadcasted_iota(jnp.int32, (8, 128), 1)
    low = jnp.zeros((8, 128), F32)
    high = jnp.zeros((8, 128), F32)
    for f in range(FIELDS):
        value = fields_ref[f]
        place = (lane >= 3 * f) & (lane < 3 * f + 3)
        low = jnp.where(place, pltpu.roll(value, 3 * f, 1) if f else value, low)
        high = jnp.where(place, pltpu.roll(value, (3 * f - 125) % 128, 1), high)
    odd_y = odd_y_ref[...] > 0
    middle_ref[...] = jnp.where(odd_y, high, low)
    pair_ref[...] = jnp.where(odd_y, low, high)


def rows_kernel(
    fields_ref, middle_ref, duo_ref, odd_y_ref, odd_ref, outer_ref, inner_ref, left_ref, right_ref
):
    odd_y = odd_y_ref[...] > 0
    pair = jnp.where(odd_y, duo_ref[0], duo_ref[1])
    right = jnp.where(odd_y, middle_ref[...], pair)
    left = jnp.where(odd_y, pair, middle_ref[...])
    left_ref[...] = left
    right_ref[...] = right
    odd = odd_ref[0:4] > 0
    for f in range(FIELDS + 2):
        value = fields_ref[f] if f < FIELDS else (right, left)[f - FIELDS]
        outer_ref[f] = jnp.where(odd, value[4:8], value[0:4])
        inner_ref[f] = jnp.where(odd, value[0:4], value[4:8])


def ahead(value, axis):
    return pltpu.roll(value, value.shape[axis] - 1, axis)


def behind(value, axis):
    return pltpu.roll(value, 1, axis)


def flat_modes(plane, after):
    s, d = plane + after, after - plane
    s1, d1 = ahead(s, 0), ahead(d, 0)
    return {"ss": s + s1, "ds": s1 - s, "sd": d + d1, "dd": d1 - d}


def flat_back(modes, rows):
    s = modes["ss"] - modes["ds"] + behind(modes["ss"] + modes["ds"], 0)
    d = modes["sd"] - modes["dd"] + behind(modes["sd"] + modes["dd"], 0)
    s, d = s[rows], d[rows]
    return s - d, s + d


def layer(lower, upper, eta):
    whole, double, four, third, two_thirds, five_thirds = eta
    modes = []
    for c in (0, 1):
        m = {}
        for xy in ("ss", "ds", "sd", "dd"):
            m[xy + "d"] = upper[c][xy] - lower[c][xy]
            if xy != "ss":
                m[xy + "s"] = upper[c][xy] + lower[c][xy]
        modes.append(m)
    low, high = [], []
    for c in (0, 1):
        u, v = modes[c], modes[1 - c]
        first, second = ("ds", "sd") if c == 0 else ("sd", "ds")
        up = {
            first + "s": double * (u[first + "s"] + u[first + "s"] + v[second + "s"]),
            second + "s": whole * (u[second + "s"] + v[first + "s"]),
            first + "d": two_thirds * (4.0 * u[first + "d"] + v[second + "d"]),
            second + "d": third * (5.0 * u[second + "d"] + v[first + "d"]),
            "dds": five_thirds * u["dds"],
            "ddd": whole * u["ddd"],
        }
        ssd = four * u["ssd"]
        lo, hi = {"ss": -ssd}, {"ss": ssd}
        for xy in ("ds", "sd", "dd"):
            lo[xy] = up[xy + "s"] - up[xy + "d"]
            hi[xy] = up[xy + "s"] + up[xy + "d"]
        low.append(lo)
        high.append(hi)
    return low, high


def krylov_kernel(
    fields_ref, left_ref, right_ref, outer_ref, both_ref, odd_ref,
    out_ref, row_ref, vec, eta, cell, after, near, far, frict, mask,
):
    lane = lax.broadcasted_iota(jnp.int32, (16, 128), 1)
    odd = odd_ref[0:4] > 0

    def joined(own, f):
        outside = outer_ref[f]
        following = jnp.where(odd, outside, both_ref[1, f])
        previous = jnp.where(odd, both_ref[0, f], outside)
        return jnp.concatenate([own, following, previous], 0)

    left = joined(left_ref[...], FIELDS + 1)
    right = joined(right_ref[...], FIELDS)

    def plane(f):
        own = joined(fields_ref[f], f)
        from_left = pltpu.roll(left, (125 - 3 * f) % 128, 1)
        from_right = pltpu.roll(right, (-3 * f) % 128, 1) if f else right
        zero = jnp.zeros((16, 128), F32)
        side = jnp.where(lane >= 125, from_left, jnp.where(lane < 3, from_right, zero))
        return jnp.concatenate([own, side], 1)

    for l in range(LEVELS):
        eta[l] = plane(2 * LEVELS + l)
    mask[...] = plane(3 * LEVELS + 1)
    frict[...] = plane(3 * LEVELS) * (1.0 / SCALE)
    for l in range(LEVELS):
        vec[0, 0, l] = plane(l)
        vec[0, 1, l] = plane(LEVELS + l)
    for l in range(LEVELS - 1):
        value = (eta[l] + eta[l + 1]) * (0.125 / SCALE / 16.0)
        cell[0, l] = value + ahead(value, 1)
    for l in range(LEVELS - 1):
        value = cell[0, l] + ahead(cell[0, l], 0)
        for n, factor in enumerate(FACTORS):
            cell[n, l] = factor * value
    for l in range(LEVELS):
        for c in (0, 1):
            vec[0, c, l] = vec[0, c, l] * mask[...]

    for k in range(3):
        shift = SHIFTS[k] / SCALE
        rows = slice(0, 16 if k < 2 else 8)

        for c in (0, 1):
            for l in range(LEVELS):
                after[c, l] = ahead(vec[k, c, l], 1)
        for side in (slice(0, 128), slice(128, 256)):
            lower, pending = None, None
            for l in range(LEVELS):
                upper = [
                    flat_modes(vec[k, c, l, :, side], after[c, l, :, side]) for c in (0, 1)
                ]
                if l:
                    eta_parts = [cell[n, l - 1, :, side] for n in range(len(FACTORS))]
                    sums, high = layer(lower, upper, eta_parts)
                    if pending is not None:
                        sums = [{m: sums[c][m] + pending[c][m] for m in sums[c]} for c in (0, 1)]
                    for c in (0, 1):
                        near[c, l - 1, rows, side], far[c, l - 1, rows, side] = flat_back(
                            sums[c], rows
                        )
                    pending = high
                lower = upper
            for c in (0, 1):
                near[c, LEVELS - 1, rows, side], far[c, LEVELS - 1, rows, side] = flat_back(
                    pending[c], rows
                )
        for c in (0, 1):
            for l in range(LEVELS):
                if k < 2:
                    image = near[c, l] + behind(far[c, l], 1)
                    value = vec[k, c, l]
                    if l == 0:
                        image = image + frict[...] * value
                    vec[k + 1, c, l] = image * mask[...] - shift * value
                else:
                    image = near[c, l, 0:8, 0:128] + behind(far[c, l, 0:8], 1)[:, 0:128]
                    value = vec[k, c, l, 0:8, 0:128]
                    if l == 0:
                        image = image + frict[0:8, 0:128] * value
                    vec[k + 1, c, l, 0:8, 0:128] = image * mask[0:8, 0:128] - shift * value

    pairs = ((0, 0), (0, 1), (0, 2), (1, 1), (1, 2), (2, 2), (1, 3), (2, 3))
    sums = [jnp.zeros((8, 128), F32) for _ in pairs]
    for c in (0, 1):
        for l in range(LEVELS):
            v = [vec[k, c, l, 0:8, 0:128] for k in range(4)]
            for k in range(4):
                out_ref[k, c, l] = v[k]
            sums = [s + v[i] * v[j] for s, (i, j) in zip(sums, pairs)]
    stacked = jnp.concatenate([jnp.sum(s, axis=0, keepdims=True) for s in sums], 0)
    totals = jnp.sum(stacked, axis=1, keepdims=True)
    ids = [lax.broadcasted_iota(jnp.int32, (8, 128), a) for a in (0, 1)]
    spread = jnp.where(ids[0] == ids[1], totals, 0.0)
    row_ref[...] = jnp.broadcast_to(jnp.sum(spread, axis=0, keepdims=True), (8, 128))


def tree(terms):
    while len(terms) > 1:
        pairs = [a + b for a, b in zip(terms[::2], terms[1::2])]
        terms = pairs + terms[2 * len(pairs) :]
    return terms[0]


def coordinates(gram):
    def dot(a, b):
        rows = []
        for i in range(len(a)):
            terms = [b[j] * gram[min(i, j), max(i, j)] for j in range(len(b))]
            rows.append(a[i] * tree(terms))
        return tree(rows)

    def added(a, b, factor):
        size = max(len(a), len(b))
        out = []
        for i in range(size):
            if i >= len(b):
                out.append(a[i])
            elif i >= len(a):
                out.append(factor * b[i])
            else:
                out.append(a[i] + factor * b[i])
        return out

    one = jnp.ones_like(gram[0, 0])
    residual, direction, answer = [one], [one], []
    norm = gram[0, 0]
    for k in range(3):
        image = [SHIFTS[i] * direction[i] for i in range(k + 1)] + [SCALE * direction[k]]
        for i in range(1, k + 1):
            image[i] = image[i] + SCALE * direction[i - 1]
        alpha = norm / dot(direction, image)
        answer = added(answer, direction, alpha)
        residual = added(residual, image, -alpha)
        if k < 2:
            fresh = dot(residual, residual)
            direction = added(residual, direction, fresh / norm)
            norm = fresh
    return answer, residual


def combine_kernel(vec_ref, rows_ref, answer_ref, residual_ref):
    row = jnp.sum(rows_ref[...], axis=0, keepdims=True)
    ids = [lax.broadcasted_iota(jnp.int32, (8, 128), a) for a in (0, 1)]
    totals = jnp.sum(jnp.where(ids[0] == ids[1], row, 0.0), axis=1, keepdims=True)
    tile = jnp.broadcast_to(totals, (8, 128))
    pairs = ((0, 0), (0, 1), (0, 2), (1, 1), (1, 2), (2, 2), (1, 3), (2, 3))
    gram = {pair: tile[n : n + 1] for n, pair in enumerate(pairs)}
    gram[0, 3] = gram[1, 2] + ((SHIFTS[0] - SHIFTS[2]) / SCALE) * gram[0, 2]
    answer, residual = coordinates(gram)
    answer = [jnp.broadcast_to(a, (8, 128)) for a in answer]
    residual = [jnp.broadcast_to(a, (8, 128)) for a in residual]
    for c in (0, 1):
        for l in range(LEVELS):
            v = [vec_ref[k, c, l] for k in range(4)]
            answer_ref[c, l] = answer[0] * v[0] + answer[1] * v[1] + answer[2] * v[2]
            residual_ref[c, l] = (
                residual[0] * v[0] + residual[1] * v[1] + residual[2] * v[2] + residual[3] * v[3]
            )


def call(kernel, outs, megabytes, *scratch, spaces=()):
    def run(*args):
        return pl.pallas_call(
            kernel,
            out_shape=tuple(outs),
            in_specs=[
                pl.BlockSpec(memory_space=spaces[n] if n < len(spaces) else VMEM)
                for n in range(len(args))
            ],
            out_specs=tuple([pl.BlockSpec(memory_space=VMEM)] * len(outs)),
            scratch_shapes=list(scratch),
            compiler_params=pltpu.CompilerParams(vmem_limit_bytes=megabytes << 20),
        )(*args)

    return run


def shape(*dims):
    return jax.ShapeDtypeStruct(dims, F32)


def everywhere(row, axes):
    size = lax.axis_size(axes)
    spread = jnp.broadcast_to(row[None], (size, 1, 128))
    return lax.all_to_all(spread, axes, 0, 0, tiled=True)


def local(*arguments):
    gx, gy = ("far", "mid", "core"), "gy"
    size_x, size_y = lax.axis_size(gx), lax.axis_size(gy)
    odd_y = jnp.full((8, 128), lax.axis_index(gy) % 2, jnp.int32)
    odd = jnp.full((8, 128), lax.axis_index("core"), jnp.int32)
    fields, to_middle, to_pair = call(
        side_kernel,
        [shape(FIELDS, 8, 128), shape(8, 128), shape(8, 128)],
        2,
        VMEM((8, 128), jnp.int32),
        pltpu.SemaphoreType.DMA((5,)),
        spaces=[pltpu.HBM] * 4,
    )(*[pltpu.with_memory_space_constraint(a, pltpu.HBM) for a in arguments], odd_y)
    middle = [(i, i + 1) for i in range(1, size_y - 1, 2)]
    middle += [(b, a) for a, b in middle]
    got_middle = lax.ppermute(to_middle, gy, middle)
    duos = [[i, i + 1] for i in range(0, size_y, 2)]
    duo = lax.all_gather(to_pair, gy, axis_index_groups=duos)
    to_outer, to_inner, left, right = call(
        rows_kernel, [shape(FIELDS + 3, 4, 128)] * 2 + [shape(8, 128)] * 2, 2
    )(fields, got_middle, duo, odd_y, odd)
    outer = [(i, i + 1) for i in range(1, size_x - 1, 2)]
    outer += [(b, a) for a, b in outer]
    got_outer = lax.ppermute(to_outer, gx, outer)
    both = lax.all_gather(to_inner, "core")
    vectors, row = call(
        krylov_kernel,
        [shape(4, 2, LEVELS, 8, 128), shape(8, 128)],
        8,
        VMEM((4, 2, LEVELS, 16, 256), F32),
        VMEM((LEVELS, 16, 256), F32),
        VMEM((len(FACTORS), LEVELS - 1, 16, 256), F32),
        VMEM((2, LEVELS, 16, 256), F32),
        VMEM((2, LEVELS, 16, 256), F32),
        VMEM((2, LEVELS, 16, 256), F32),
        VMEM((16, 256), F32),
        VMEM((16, 256), F32),
    )(fields, left, right, got_outer, both, odd)
    row = jnp.sum(everywhere(row[0:1], ("mid", "core")), axis=0)
    rows = everywhere(row, ("far", "gy"))[:, 0]
    return call(combine_kernel, [shape(2, LEVELS, 8, 128)] * 2, 4)(vectors, rows)


def solution(mesh):
    size_x, size_y = mesh.devices.shape
    split = Mesh(mesh.devices.reshape(8, size_x // 16, 2, size_y), ("far", "mid", "core", "gy"))
    gx = ("far", "mid", "core")
    vector, plane = P(None, None, gx, "gy"), P(gx, "gy")
    return jax.shard_map(
        local,
        mesh=split,
        in_specs=(vector, P(None, gx, "gy"), plane, plane),
        out_specs=(vector, vector),
        check_vma=False,
    )
```

```python
import jax
import jax.numpy as jnp
from jax import lax
from jax.experimental import pallas as pl
from jax.experimental.pallas import tpu as pltpu
from jax.sharding import Mesh, PartitionSpec as P

LEVELS = 11
FIELDS = 3 * LEVELS + 2
SCALE = 16.0
SHIFTS = (8.0, 2.0, 20.0)
FACTORS = (1.0, 2.0, 4.0, 1.0 / 3.0, 2.0 / 3.0, 5.0 / 3.0)
F32 = jnp.float32
VMEM = pltpu.VMEM


def side_kernel(
    src_ref, eta_ref, fric_ref, mask_ref, odd_y_ref, fields_ref, middle_ref, pair_ref, mask, sems
):
    parts = [
        (src_ref.at[0], fields_ref.at[0:LEVELS]),
        (src_ref.at[1], fields_ref.at[LEVELS : 2 * LEVELS]),
        (eta_ref, fields_ref.at[2 * LEVELS : 3 * LEVELS]),
        (fric_ref, fields_ref.at[3 * LEVELS]),
        (mask_ref, mask),
    ]
    copies = [pltpu.make_async_copy(a, b, sems.at[n]) for n, (a, b) in enumerate(parts)]
    for copy in copies:
        copy.start()
    for copy in copies:
        copy.wait()
    fields_ref[FIELDS - 1] = mask[...].astype(F32)
    lane = lax.broadcasted_iota(jnp.int32, (8, 128), 1)
    low = jnp.zeros((8, 128), F32)
    high = jnp.zeros((8, 128), F32)
    for f in range(FIELDS):
        value = fields_ref[f]
        place = (lane >= 3 * f) & (lane < 3 * f + 3)
        low = jnp.where(place, pltpu.roll(value, 3 * f, 1) if f else value, low)
        high = jnp.where(place, pltpu.roll(value, (3 * f - 125) % 128, 1), high)
    odd_y = odd_y_ref[...] > 0
    middle_ref[...] = jnp.where(odd_y, high, low)
    pair_ref[...] = jnp.where(odd_y, low, high)


def rows_kernel(
    fields_ref, middle_ref, duo_ref, odd_y_ref, odd_ref, outer_ref, inner_ref, left_ref, right_ref
):
    odd_y = odd_y_ref[...] > 0
    pair = jnp.where(odd_y, duo_ref[0], duo_ref[1])
    right = jnp.where(odd_y, middle_ref[...], pair)
    left = jnp.where(odd_y, pair, middle_ref[...])
    left_ref[...] = left
    right_ref[...] = right
    odd = odd_ref[0:4] > 0
    for f in range(FIELDS + 2):
        value = fields_ref[f] if f < FIELDS else (right, left)[f - FIELDS]
        outer_ref[f] = jnp.where(odd, value[4:8], value[0:4])
        inner_ref[f] = jnp.where(odd, value[0:4], value[4:8])


def ahead(value, axis):
    return pltpu.roll(value, value.shape[axis] - 1, axis)


def behind(value, axis):
    return pltpu.roll(value, 1, axis)


def flat_modes(plane, after):
    s, d = plane + after, after - plane
    s1, d1 = ahead(s, 0), ahead(d, 0)
    return {"ss": s + s1, "ds": s1 - s, "sd": d + d1, "dd": d1 - d}


def flat_back(modes, rows):
    s = modes["ss"] - modes["ds"] + behind(modes["ss"] + modes["ds"], 0)
    d = modes["sd"] - modes["dd"] + behind(modes["sd"] + modes["dd"], 0)
    s, d = s[rows], d[rows]
    return s - d, s + d


def layer(lower, upper, eta):
    whole, double, four, third, two_thirds, five_thirds = eta
    modes = []
    for c in (0, 1):
        m = {}
        for xy in ("ss", "ds", "sd", "dd"):
            m[xy + "d"] = upper[c][xy] - lower[c][xy]
            if xy != "ss":
                m[xy + "s"] = upper[c][xy] + lower[c][xy]
        modes.append(m)
    low, high = [], []
    for c in (0, 1):
        u, v = modes[c], modes[1 - c]
        first, second = ("ds", "sd") if c == 0 else ("sd", "ds")
        up = {
            first + "s": double * (u[first + "s"] + u[first + "s"] + v[second + "s"]),
            second + "s": whole * (u[second + "s"] + v[first + "s"]),
            first + "d": two_thirds * (4.0 * u[first + "d"] + v[second + "d"]),
            second + "d": third * (5.0 * u[second + "d"] + v[first + "d"]),
            "dds": five_thirds * u["dds"],
            "ddd": whole * u["ddd"],
        }
        ssd = four * u["ssd"]
        lo, hi = {"ss": -ssd}, {"ss": ssd}
        for xy in ("ds", "sd", "dd"):
            lo[xy] = up[xy + "s"] - up[xy + "d"]
            hi[xy] = up[xy + "s"] + up[xy + "d"]
        low.append(lo)
        high.append(hi)
    return low, high


def krylov_kernel(
    fields_ref, left_ref, right_ref, outer_ref, both_ref, odd_ref,
    out_ref, row_ref, vec, eta, cell, after, near, far, frict, mask,
):
    lane = lax.broadcasted_iota(jnp.int32, (16, 128), 1)
    odd = odd_ref[0:4] > 0

    def joined(own, f):
        outside = outer_ref[f]
        following = jnp.where(odd, outside, both_ref[1, f])
        previous = jnp.where(odd, both_ref[0, f], outside)
        return jnp.concatenate([own, following, previous], 0)

    left = joined(left_ref[...], FIELDS + 1)
    right = joined(right_ref[...], FIELDS)

    def plane(f):
        own = joined(fields_ref[f], f)
        from_left = pltpu.roll(left, (125 - 3 * f) % 128, 1)
        from_right = pltpu.roll(right, (-3 * f) % 128, 1) if f else right
        zero = jnp.zeros((16, 128), F32)
        side = jnp.where(lane >= 125, from_left, jnp.where(lane < 3, from_right, zero))
        return jnp.concatenate([own, side], 1)

    for l in range(LEVELS):
        eta[l] = plane(2 * LEVELS + l)
    mask[...] = plane(3 * LEVELS + 1)
    frict[...] = plane(3 * LEVELS) * (1.0 / SCALE)
    for l in range(LEVELS):
        vec[0, 0, l] = plane(l)
        vec[0, 1, l] = plane(LEVELS + l)
    for l in range(LEVELS - 1):
        value = (eta[l] + eta[l + 1]) * (0.125 / SCALE / 16.0)
        cell[0, l] = value + ahead(value, 1)
    for l in range(LEVELS - 1):
        value = cell[0, l] + ahead(cell[0, l], 0)
        for n, factor in enumerate(FACTORS):
            cell[n, l] = factor * value
    for l in range(LEVELS):
        for c in (0, 1):
            vec[0, c, l] = vec[0, c, l] * mask[...]

    for k in range(3):
        shift = SHIFTS[k] / SCALE
        rows = slice(0, 16 if k < 2 else 8)

        for c in (0, 1):
            for l in range(LEVELS):
                after[c, l] = ahead(vec[k, c, l], 1)
        for side in (slice(0, 128), slice(128, 256)):
            lower, pending = None, None
            for l in range(LEVELS):
                upper = [
                    flat_modes(vec[k, c, l, :, side], after[c, l, :, side]) for c in (0, 1)
                ]
                if l:
                    eta_parts = [cell[n, l - 1, :, side] for n in range(len(FACTORS))]
                    sums, high = layer(lower, upper, eta_parts)
                    if pending is not None:
                        sums = [{m: sums[c][m] + pending[c][m] for m in sums[c]} for c in (0, 1)]
                    for c in (0, 1):
                        near[c, l - 1, rows, side], far[c, l - 1, rows, side] = flat_back(
                            sums[c], rows
                        )
                    pending = high
                lower = upper
            for c in (0, 1):
                near[c, LEVELS - 1, rows, side], far[c, LEVELS - 1, rows, side] = flat_back(
                    pending[c], rows
                )
        for c in (0, 1):
            for l in range(LEVELS):
                if k < 2:
                    image = near[c, l] + behind(far[c, l], 1)
                    value = vec[k, c, l]
                    if l == 0:
                        image = image + frict[...] * value
                    vec[k + 1, c, l] = image * mask[...] - shift * value
                else:
                    image = near[c, l, 0:8, 0:128] + behind(far[c, l, 0:8], 1)[:, 0:128]
                    value = vec[k, c, l, 0:8, 0:128]
                    if l == 0:
                        image = image + frict[0:8, 0:128] * value
                    out_ref[3, c, l] = image * mask[0:8, 0:128] - shift * value

    pairs = ((0, 0), (0, 1), (0, 2), (1, 1), (1, 2), (2, 2), (1, 3), (2, 3))
    sums = [jnp.zeros((8, 128), F32) for _ in pairs]
    for c in (0, 1):
        for l in range(LEVELS):
            v = [vec[k, c, l, 0:8, 0:128] for k in range(3)]
            for k in range(3):
                out_ref[k, c, l] = v[k]
            v.append(out_ref[3, c, l])
            sums = [s + v[i] * v[j] for s, (i, j) in zip(sums, pairs)]
    stacked = jnp.concatenate([jnp.sum(s, axis=0, keepdims=True) for s in sums], 0)
    totals = jnp.sum(stacked, axis=1, keepdims=True)
    ids = [lax.broadcasted_iota(jnp.int32, (8, 128), a) for a in (0, 1)]
    spread = jnp.where(ids[0] == ids[1], totals, 0.0)
    row_ref[...] = jnp.broadcast_to(jnp.sum(spread, axis=0, keepdims=True), (8, 128))


def tree(terms):
    while len(terms) > 1:
        pairs = [a + b for a, b in zip(terms[::2], terms[1::2])]
        terms = pairs + terms[2 * len(pairs) :]
    return terms[0]


def coordinates(gram):
    def dot(a, b):
        rows = []
        for i in range(len(a)):
            terms = [b[j] * gram[min(i, j), max(i, j)] for j in range(len(b))]
            rows.append(a[i] * tree(terms))
        return tree(rows)

    def added(a, b, factor):
        size = max(len(a), len(b))
        out = []
        for i in range(size):
            if i >= len(b):
                out.append(a[i])
            elif i >= len(a):
                out.append(factor * b[i])
            else:
                out.append(a[i] + factor * b[i])
        return out

    one = jnp.ones_like(gram[0, 0])
    residual, direction, answer = [one], [one], []
    norm = gram[0, 0]
    for k in range(3):
        image = [SHIFTS[i] * direction[i] for i in range(k + 1)] + [SCALE * direction[k]]
        for i in range(1, k + 1):
            image[i] = image[i] + SCALE * direction[i - 1]
        alpha = norm / dot(direction, image)
        answer = added(answer, direction, alpha)
        residual = added(residual, image, -alpha)
        if k < 2:
            fresh = dot(residual, residual)
            direction = added(residual, direction, fresh / norm)
            norm = fresh
    return answer, residual


def combine_kernel(vec_ref, rows_ref, answer_ref, residual_ref):
    row = jnp.sum(rows_ref[...], axis=0, keepdims=True)
    ids = [lax.broadcasted_iota(jnp.int32, (8, 128), a) for a in (0, 1)]
    totals = jnp.sum(jnp.where(ids[0] == ids[1], row, 0.0), axis=1, keepdims=True)
    tile = jnp.broadcast_to(totals, (8, 128))
    pairs = ((0, 0), (0, 1), (0, 2), (1, 1), (1, 2), (2, 2), (1, 3), (2, 3))
    gram = {pair: tile[n : n + 1] for n, pair in enumerate(pairs)}
    gram[0, 3] = gram[1, 2] + ((SHIFTS[0] - SHIFTS[2]) / SCALE) * gram[0, 2]
    answer, residual = coordinates(gram)
    answer = [jnp.broadcast_to(a, (8, 128)) for a in answer]
    residual = [jnp.broadcast_to(a, (8, 128)) for a in residual]
    for c in (0, 1):
        for l in range(LEVELS):
            v = [vec_ref[k, c, l] for k in range(4)]
            answer_ref[c, l] = answer[0] * v[0] + answer[1] * v[1] + answer[2] * v[2]
            residual_ref[c, l] = (
                residual[0] * v[0] + residual[1] * v[1] + residual[2] * v[2] + residual[3] * v[3]
            )


def call(kernel, outs, megabytes, *scratch, spaces=()):
    def run(*args):
        return pl.pallas_call(
            kernel,
            out_shape=tuple(outs),
            in_specs=[
                pl.BlockSpec(memory_space=spaces[n] if n < len(spaces) else VMEM)
                for n in range(len(args))
            ],
            out_specs=tuple([pl.BlockSpec(memory_space=VMEM)] * len(outs)),
            scratch_shapes=list(scratch),
            compiler_params=pltpu.CompilerParams(vmem_limit_bytes=megabytes << 20),
        )(*args)

    return run


def shape(*dims):
    return jax.ShapeDtypeStruct(dims, F32)


def everywhere(row, axes):
    size = lax.axis_size(axes)
    spread = jnp.broadcast_to(row[None], (size, 1, 128))
    return lax.all_to_all(spread, axes, 0, 0, tiled=True)


def local(*arguments):
    gx, gy = ("far", "mid", "core"), "gy"
    size_x, size_y = lax.axis_size(gx), lax.axis_size(gy)
    odd_y = jnp.full((8, 128), lax.axis_index(gy) % 2, jnp.int32)
    odd = jnp.full((8, 128), lax.axis_index("core"), jnp.int32)
    fields, to_middle, to_pair = call(
        side_kernel,
        [shape(FIELDS, 8, 128), shape(8, 128), shape(8, 128)],
        2,
        VMEM((8, 128), jnp.int32),
        pltpu.SemaphoreType.DMA((5,)),
        spaces=[pltpu.HBM] * 4,
    )(*[pltpu.with_memory_space_constraint(a, pltpu.HBM) for a in arguments], odd_y)
    middle = [(i, i + 1) for i in range(1, size_y - 1, 2)]
    middle += [(b, a) for a, b in middle]
    got_middle = lax.ppermute(to_middle, gy, middle)
    duos = [[i, i + 1] for i in range(0, size_y, 2)]
    duo = lax.all_gather(to_pair, gy, axis_index_groups=duos)
    to_outer, to_inner, left, right = call(
        rows_kernel, [shape(FIELDS + 3, 4, 128)] * 2 + [shape(8, 128)] * 2, 2
    )(fields, got_middle, duo, odd_y, odd)
    outer = [(i, i + 1) for i in range(1, size_x - 1, 2)]
    outer += [(b, a) for a, b in outer]
    got_outer = lax.ppermute(to_outer, gx, outer)
    both = lax.all_gather(to_inner, "core")
    vectors, row = call(
        krylov_kernel,
        [shape(4, 2, LEVELS, 8, 128), shape(8, 128)],
        8,
        VMEM((3, 2, LEVELS, 16, 256), F32),
        VMEM((LEVELS, 16, 256), F32),
        VMEM((len(FACTORS), LEVELS - 1, 16, 256), F32),
        VMEM((2, LEVELS, 16, 256), F32),
        VMEM((2, LEVELS, 16, 256), F32),
        VMEM((2, LEVELS, 16, 256), F32),
        VMEM((16, 256), F32),
        VMEM((16, 256), F32),
    )(fields, left, right, got_outer, both, odd)
    row = jnp.sum(everywhere(row[0:1], ("mid", "core")), axis=0)
    rows = everywhere(row, ("far", "gy"))[:, 0]
    return call(combine_kernel, [shape(2, LEVELS, 8, 128)] * 2, 4)(vectors, rows)


def solution(mesh):
    size_x, size_y = mesh.devices.shape
    split = Mesh(mesh.devices.reshape(8, size_x // 16, 2, size_y), ("far", "mid", "core", "gy"))
    gx = ("far", "mid", "core")
    vector, plane = P(None, None, gx, "gy"), P(gx, "gy")
    return jax.shard_map(
        local,
        mesh=split,
        in_specs=(vector, P(None, gx, "gy"), plane, plane),
        out_specs=(vector, vector),
        check_vma=False,
    )
```
